32 devices in a mesh: ctx: 16 (over z, x, core), ch: 2 (over y).
Axes of the slice: x: 2, y: 2, z: 4, core: 2. Of those that a mesh axis runs over, the one named last changes fastest.
Arguments:
- qkv: bfloat16 [3, 512, 4096], P(None, None, ('ctx', 'ch')), may hold values from -6 to 6
- conv_taps: float32 [3, 512, 7], replicated, may hold values from -2 to 2
- filters: float32 [512, 4096], P('ch', 'ctx'), may hold values from -0.09375 to 0.09375
- skip: float32 [512], P('ch'), may hold values from -4 to 4
Outputs:
- mixed: bfloat16 [512, 4096], P('ch', 'ctx')
The draws below stay inside these ranges and needn't reach their ends.
All inputs are finite; a program needn't handle non-finite values.
Results may differ from the reference program's by a relative error of at most 0.013.
Values may be sent and summed in bfloat16 or wider, within the bound.
A program may use at most 64 MiB of HBM per device.

```python
import math
import jax
import jax.numpy as jnp
from jax import lax

C = 512
TAPS = 7
SEQ = 4096


def block_scale(key, extent, pieces, smallest, top_value):
    factor_of = 1.0
    for position, shards_of in pieces:
        steps = jax.random.uniform(jax.random.fold_in(jax.random.fold_in(key, 6), position), (shards_of,), jnp.float32, smallest / len(pieces), top_value / len(pieces))
        factor_of = factor_of * jnp.repeat(jnp.exp(steps), extent[position] // shards_of).reshape((-1,) + (1,) * (len(extent) - 1 - position))
    return factor_of


def normal_values(stream_key, shape, scale, limit, shards=(), kind=jnp.bfloat16):
    values = scale * jax.random.normal(stream_key, shape, jnp.float32)
    if shards:
        values = values * block_scale(stream_key, shape, shards, -0.22, 0.18)
    return jnp.clip(values, -limit, limit).astype(kind)


def setup_inputs(seed: int = 0) -> dict:
    key_list = jax.random.split(jax.random.key(seed), 5)
    qkv = normal_values(key_list[0], (3, C, SEQ), 1.0, 6.0, ((2, 32),))
    conv_taps = normal_values(key_list[1], (3, C, TAPS), TAPS ** -0.5, 2.0, (), jnp.float32)
    filters = normal_values(key_list[2], (C, SEQ), SEQ ** -0.5, 0.09375, ((0, 2), (1, 16)), jnp.float32)
    skip = normal_values(key_list[3], (C,), 1.0, 4.0, ((0, 2),), jnp.float32)
    return dict(qkv=qkv, conv_taps=conv_taps, filters=filters, skip=skip)


def featurize(stream, taps):
    reach = taps.shape[2] - 1
    length = stream.shape[2]
    padded = jnp.pad(stream.astype(jnp.float32), ((0, 0), (0, 0), (reach, 0)))
    total = jnp.zeros(stream.shape, jnp.float32)
    for offset in range(taps.shape[2]):
        total = total + taps[:, :, offset:offset + 1] * padded[:, :, reach - offset:reach - offset + length]
    return total


def reference(qkv, conv_taps, filters, skip):
    group = math.gcd(C, 32)
    count = C // group
    stream_blocks = qkv.reshape(3, count, group, SEQ).transpose(1, 0, 2, 3)
    tap_blocks = conv_taps.reshape(3, count, group, TAPS).transpose(1, 0, 2, 3)
    filter_blocks = filters.reshape(count, group, SEQ)
    skip_blocks = skip.reshape(count, group)

    def one_block(items):
        stream, taps, filt, direct = items
        features = featurize(stream, taps)
        query = lax.optimization_barrier(features[0].astype(jnp.bfloat16))
        gated = lax.optimization_barrier((features[1] * features[2]).astype(jnp.bfloat16))
        signal = gated.astype(jnp.float32)
        size = 2 * SEQ
        spectrum = jnp.fft.rfft(signal, n=size, axis=-1) * jnp.fft.rfft(filt, n=size, axis=-1)
        long_conv = jnp.fft.irfft(spectrum, n=size, axis=-1)[:, :SEQ]
        mixed = query.astype(jnp.float32) * (long_conv + direct[:, None] * signal)
        return mixed.astype(jnp.bfloat16)

    result = lax.map(one_block, (stream_blocks, tap_blocks, filter_blocks, skip_blocks))
    return result.reshape(C, SEQ)
```

```python
import functools
import math

import jax
import jax.numpy as jnp
import ml_dtypes
import numpy as np
from jax import lax
from jax.experimental import pallas as pl
from jax.experimental.pallas import tpu as pltpu
from jax.sharding import PartitionSpec as P

MESH = pl.DeviceIdType.MESH
F32 = jnp.float32
BF16 = jnp.bfloat16


def tables(devices, width, chans):
    total = 2 * devices * width
    a = np.arange(devices)
    k1 = np.arange(devices) + 0.5
    eye = np.eye(chans)
    angle = 2 * np.pi * np.outer(k1, a) / (2 * devices)
    forward = np.concatenate([np.kron(np.cos(angle), eye), np.kron(-np.sin(angle), eye)], 0)
    inverse = np.concatenate([np.kron(np.cos(angle.T), eye), np.kron(-np.sin(angle.T), eye)], 1)
    inverse = inverse * (2.0 / total)
    b = np.arange(width)
    turn = 2 * np.pi * np.outer(k1, b) / total
    twist = np.stack([np.cos(turn), np.sin(turn)])
    inner = 2 * np.pi * (np.outer(b, b) % width) / width
    cos, sin = np.cos(inner), np.sin(inner)
    wide = np.stack(
        [np.block([[cos, -sin], [sin, cos]]), np.block([[cos, sin], [-sin, cos]])]
    )
    low = lambda x: jnp.asarray(x.astype(ml_dtypes.bfloat16))
    return (
        low(forward),
        low(inverse),
        low(wide),
        jnp.asarray(twist.astype(np.float32)[:, :, None, :]),
    )


def kernel(
    lanes, groups, reach,
    qkv, taps, filters, skip, fwd_hbm, inv_hbm, wide_hbm, twist_hbm,
    out,
    kvbuf, qbuf, fraw, fsend, fbuf, tapv, tapb, skipb, fwd, inv, wide, twist,
    gbuf, hspec, vbuf, mbuf,
    load_sem, own_sem, send_sem, recv_sem,
):
    devices = lanes * groups
    chans = fbuf.shape[1]
    width = fbuf.shape[2]
    mine = lax.axis_index("ctx")
    side = lax.axis_index("ch")
    me = mine * groups + side
    per_side = lanes * chans

    def rows_of(i, j):
        return pl.ds(pl.multiple_of(j * per_side + i * chans, chans), chans)

    def side_rows(i):
        return pl.ds(pl.multiple_of(i * chans, chans), chans)

    load_f = pltpu.make_async_copy(filters, fraw, load_sem.at[0])
    load_f.start()
    own_rows = rows_of(mine, side)
    loads = [
        pltpu.make_async_copy(taps.at[:, own_rows], tapv, load_sem.at[1]),
        pltpu.make_async_copy(fwd_hbm, fwd, load_sem.at[2]),
        pltpu.make_async_copy(wide_hbm, wide, load_sem.at[3]),
        pltpu.make_async_copy(twist_hbm, twist, load_sem.at[4]),
        pltpu.make_async_copy(inv_hbm, inv, load_sem.at[5]),
    ]
    own_kv = pltpu.make_async_copy(
        qkv.at[pl.ds(1, 2), own_rows], kvbuf.at[:, me + 1], own_sem.at[0]
    )
    own_q = pltpu.make_async_copy(qkv.at[0, own_rows], qbuf.at[me + 1], own_sem.at[1])
    own_kv.start()
    own_q.start()
    for load in loads:
        load.start()

    barrier = pltpu.get_barrier_semaphore()

    def greet(d, carry):
        t = lax.rem(me + d, devices)
        pl.semaphore_signal(
            barrier, inc=1, device_id=(t // groups, t % groups), device_id_type=MESH
        )
        return carry

    lax.fori_loop(1, devices, greet, 0)

    kvbuf[0, 0] = jnp.zeros((chans, width), BF16)
    kvbuf[1, 0] = jnp.zeros((chans, width), BF16)
    qbuf[0] = jnp.zeros((chans, width), BF16)
    load_f.wait()
    for g in range(groups):
        fsend[g] = fraw[:, g * width : (g + 1) * width].astype(BF16)

    pl.semaphore_wait(barrier, devices - 1)

    def send_filters(d, carry):
        i = lax.rem(mine + d, lanes)
        pltpu.make_async_remote_copy(
            src_ref=fsend.at[:, side_rows(i)],
            dst_ref=fbuf.at[pl.ds(mine * groups, groups)],
            send_sem=send_sem.at[0], recv_sem=recv_sem.at[0],
            device_id=(i, side), device_id_type=MESH,
        ).start()
        return carry

    def send_kv(d, carry):
        t = lax.rem(me + d, devices)
        i, j = t // groups, t % groups
        pltpu.make_async_remote_copy(
            src_ref=qkv.at[pl.ds(1, 2), rows_of(i, j)],
            dst_ref=kvbuf.at[:, me + 1],
            send_sem=send_sem.at[1], recv_sem=recv_sem.at[1],
            device_id=(i, j), device_id_type=MESH,
        ).start()
        return carry

    def send_q(d, carry):
        t = lax.rem(me + d, devices)
        i, j = t // groups, t % groups
        pltpu.make_async_remote_copy(
            src_ref=qkv.at[0, rows_of(i, j)],
            dst_ref=qbuf.at[me + 1],
            send_sem=send_sem.at[2], recv_sem=recv_sem.at[2],
            device_id=(i, j), device_id_type=MESH,
        ).start()
        return carry

    lax.fori_loop(1, lanes, send_filters, 0)
    lax.fori_loop(1, devices, send_kv, 0)
    lax.fori_loop(1, devices, send_q, 0)
    own_f = pltpu.make_async_copy(
        fsend.at[:, side_rows(mine)], fbuf.at[pl.ds(mine * groups, groups)], own_sem.at[2]
    )
    own_f.start()

    for load in loads:
        load.wait()
    for s in range(3):
        for i in range(reach + 1):
            tapb[s, i] = jnp.broadcast_to(tapv[s, :, i : i + 1], (chans, width))
    pick = lax.broadcasted_iota(jnp.int32, (chans, per_side), 1) == (
        mine * chans + lax.broadcasted_iota(jnp.int32, (chans, per_side), 0)
    )
    column = jnp.sum(jnp.where(pick, skip[...], 0.0), axis=1, keepdims=True)
    skipb[...] = jnp.broadcast_to(column, (chans, width))

    step = 8
    block = step * chans
    half = devices * chans

    def dot(left, right):
        return jnp.dot(left, right, preferred_element_type=F32)

    def forward(signal, r0, k0):
        real = dot(fwd[pl.ds(r0, block), :], signal).reshape(step, chans, width)
        imag = dot(fwd[pl.ds(half + r0, block), :], signal).reshape(step, chans, width)
        cos, sin = twist[0, pl.ds(k0, step)], twist[1, pl.ds(k0, step)]
        turned = jnp.concatenate(
            [
                (real * cos + imag * sin).astype(BF16).reshape(block, width),
                (imag * cos - real * sin).astype(BF16).reshape(block, width),
            ],
            axis=1,
        )
        return dot(turned, wide[0])

    own_f.wait()
    got_f = fbuf.at[pl.ds(0, devices - groups)]
    pltpu.make_async_copy(got_f, got_f, recv_sem.at[0]).wait()

    @pl.loop(0, devices // step)
    def _(n):
        r0 = pl.multiple_of(n * block, block)
        hspec[pl.ds(r0, block), :] = forward(
            fbuf[...].reshape(half, width), r0, n * step
        )

    own_kv.wait()
    got_kv = kvbuf.at[:, pl.ds(0, devices - 1)]
    pltpu.make_async_copy(got_kv, got_kv, recv_sem.at[1]).wait()
    fstep = 4
    lane = lax.broadcasted_iota(jnp.int32, (fstep * chans, width), 1)

    def feature(stream, cur, prev):
        cur = cur.astype(F32).reshape(fstep * chans, width)
        prev = prev.astype(F32).reshape(fstep * chans, width)
        acc = tapb[stream, 0] * cur.reshape(fstep, chans, width)
        for i in range(1, reach + 1):
            moved = pltpu.roll(jnp.where(lane >= width - i, prev, cur), i, 1)
            acc = acc + tapb[stream, i] * moved.reshape(fstep, chans, width)
        return acc

    @pl.loop(0, devices // fstep)
    def _(n):
        a0 = n * fstep
        key = feature(1, kvbuf[0, pl.ds(a0 + 1, fstep)], kvbuf[0, pl.ds(a0, fstep)])
        value = feature(2, kvbuf[1, pl.ds(a0 + 1, fstep)], kvbuf[1, pl.ds(a0, fstep)])
        gbuf[pl.ds(a0, fstep)] = (key * value).astype(BF16)

    @pl.loop(0, devices // step)
    def _(n):
        r0 = pl.multiple_of(n * block, block)
        spec = forward(gbuf[...].reshape(half, width), r0, n * step)
        filt = hspec[pl.ds(r0, block), :]
        sr, si = spec[:, :width], spec[:, width:]
        fr, fi = filt[:, :width], filt[:, width:]
        prod = jnp.concatenate(
            [(sr * fr - si * fi).astype(BF16), (sr * fi + si * fr).astype(BF16)], axis=1
        )
        back = dot(prod, wide[1])
        br = back[:, :width].reshape(step, chans, width)
        bi = back[:, width:].reshape(step, chans, width)
        cos, sin = twist[0, pl.ds(n * step, step)], twist[1, pl.ds(n * step, step)]
        vbuf[pl.ds(r0, block), :] = (br * cos - bi * sin).astype(BF16).reshape(block, width)
        vbuf[pl.ds(half + r0, block), :] = (
            (br * sin + bi * cos).astype(BF16).reshape(block, width)
        )

    own_q.wait()
    got_q = qbuf.at[pl.ds(0, devices - 1)]
    pltpu.make_async_copy(got_q, got_q, recv_sem.at[2]).wait()

    @pl.loop(0, devices // fstep)
    def _(n):
        a0 = n * fstep
        rows = pl.ds(pl.multiple_of(a0 * chans, fstep * chans), fstep * chans)
        query = feature(0, qbuf[pl.ds(a0 + 1, fstep)], qbuf[pl.ds(a0, fstep)])
        query = query.astype(BF16).astype(F32)
        conv = dot(inv[rows, :], vbuf[...]).reshape(fstep, chans, width)
        signal = gbuf[pl.ds(a0, fstep)].astype(F32)
        mbuf[pl.ds(a0, fstep)] = (query * (conv + skipb[...] * signal)).astype(BF16)

    def send_out(d, carry):
        i = lax.rem(mine + d, lanes)
        pltpu.make_async_remote_copy(
            src_ref=mbuf.at[pl.ds(i * groups, groups)],
            dst_ref=out.at[:, side_rows(mine)],
            send_sem=send_sem.at[3], recv_sem=recv_sem.at[3],
            device_id=(i, side), device_id_type=MESH,
        ).start()
        return carry

    lax.fori_loop(1, lanes, send_out, 0)
    own_o = pltpu.make_async_copy(
        mbuf.at[pl.ds(mine * groups, groups)], out.at[:, side_rows(mine)], own_sem.at[3]
    )
    own_o.start()

    sent_f = fbuf.at[pl.ds(0, devices - groups)]
    pltpu.make_async_copy(sent_f, sent_f, send_sem.at[0]).wait()
    pltpu.make_async_copy(got_kv, got_kv, send_sem.at[1]).wait()
    pltpu.make_async_copy(got_q, got_q, send_sem.at[2]).wait()
    got_o = mbuf.at[pl.ds(0, devices - groups)]
    pltpu.make_async_copy(got_o, got_o, send_sem.at[3]).wait()
    own_o.wait()
    pltpu.make_async_copy(got_o, got_o, recv_sem.at[3]).wait()


def fused_local(lanes, groups, qkv, conv_taps, filters, skip):
    devices = lanes * groups
    channels, width = qkv.shape[1], qkv.shape[2]
    chans = channels // devices
    count = conv_taps.shape[2]
    fwd, inv, wide, twist = tables(devices, width, chans)
    any_spec = pl.BlockSpec(memory_space=pl.ANY)
    vmem_spec = pl.BlockSpec(memory_space=pltpu.VMEM)
    per_side = lanes * chans
    landed = pl.pallas_call(
        functools.partial(kernel, lanes, groups, count - 1),
        out_shape=jax.ShapeDtypeStruct((groups, per_side, width), BF16),
        in_specs=[any_spec, any_spec, any_spec, vmem_spec] + [any_spec] * 4,
        out_specs=any_spec,
        scratch_shapes=[
            pltpu.VMEM((2, devices + 1, chans, width), BF16),
            pltpu.VMEM((devices + 1, chans, width), BF16),
            pltpu.VMEM(filters.shape, F32),
            pltpu.VMEM((groups, per_side, width), BF16),
            pltpu.VMEM((devices, chans, width), BF16),
            pltpu.VMEM((3, chans, count), F32),
            pltpu.VMEM((3, count, chans, width), F32),
            pltpu.VMEM((chans, width), F32),
            pltpu.VMEM(fwd.shape, BF16),
            pltpu.VMEM(inv.shape, BF16),
            pltpu.VMEM(wide.shape, BF16),
            pltpu.VMEM(twist.shape, F32),
            pltpu.VMEM((devices, chans, width), BF16),
            pltpu.VMEM((channels, 2 * width), F32),
            pltpu.VMEM((2 * channels, width), BF16),
            pltpu.VMEM((devices, chans, width), BF16),
            pltpu.SemaphoreType.DMA((6,)),
            pltpu.SemaphoreType.DMA((4,)),
            pltpu.SemaphoreType.DMA((4,)),
            pltpu.SemaphoreType.DMA((4,)),
        ],
        compiler_params=pltpu.CompilerParams(
            collective_id=0, has_side_effects=True, vmem_limit_bytes=32 * 1024 * 1024
        ),
    )(qkv, conv_taps, filters, skip.reshape(1, -1), fwd, inv, wide, twist)
    return landed.transpose(1, 0, 2).reshape(per_side, groups * width)


def from_behind(shard, axis, by):
    length = lax.axis_size(axis)
    pairs = [(i, i + by) for i in range(length) if 0 <= i + by < length]
    return lax.ppermute(shard, axis, pairs)


def featurize(block, earlier, taps):
    reach = taps.shape[2] - 1
    length = block.shape[2]
    joined = jnp.concatenate([earlier, block], axis=2).astype(jnp.float32)
    total = jnp.zeros(block.shape, jnp.float32)
    for offset in range(taps.shape[2]):
        total = (
            total
            + taps[:, :, offset : offset + 1]
            * joined[:, :, reach - offset : reach - offset + length]
        )
    query = lax.optimization_barrier(total[0].astype(jnp.bfloat16))
    gated = lax.optimization_barrier((total[1] * total[2]).astype(jnp.bfloat16))
    return (query, gated)


def phase(product, modulus, sign):
    angle = sign * 2.0 * math.pi / modulus * (product % modulus).astype(jnp.float32)
    return (jnp.cos(angle), jnp.sin(angle))


def dft_table(index_in, index_out, modulus, sign):
    cosine, sine = phase(index_in[:, None] * index_out[None, :], modulus, sign)
    return jnp.stack([jnp.stack([cosine, sine]), jnp.stack([-sine, cosine])])


def complex_times(left, right):
    return jnp.stack(
        [left[0] * right[0] - left[1] * right[1], left[0] * right[1] + left[1] * right[0]]
    )


def twisted(values, cosine, sine):
    return jnp.stack([values[0] * cosine - values[1] * sine, values[0] * sine + values[1] * cosine])


def local_transform(values, sign):
    highest = lax.Precision.HIGHEST
    length = values.shape[-1]
    first = max((d for d in range(1, math.isqrt(length) + 1) if length % d == 0))
    second = length // first
    lead = values.shape[:-1]
    shaped = values.reshape(lead + (first, second))
    index_a = jnp.arange(first, dtype=jnp.int32)
    index_b = jnp.arange(second, dtype=jnp.int32)
    outer = dft_table(index_a, index_a, first, sign)
    part = jnp.einsum("p...ab,pqak->q...kb", shaped, outer, precision=highest)
    twist_c, twist_s = phase(index_a[:, None] * index_b[None, :], length, sign)
    part = twisted(part, twist_c, twist_s)
    inner = dft_table(index_b, index_b, second, sign)
    result = jnp.einsum("p...kb,pqbm->q...mk", part, inner, precision=highest)
    return result.reshape(lead + (length,))


def to_columns(values):
    return lax.all_to_all(
        values.astype(jnp.bfloat16), "ctx", split_axis=3, concat_axis=2, tiled=True
    ).astype(values.dtype)


def to_rows(values):
    return lax.all_to_all(
        values.astype(jnp.bfloat16), "ctx", split_axis=2, concat_axis=3, tiled=True
    ).astype(values.dtype)


def spread_conv(signal, filters):
    highest = lax.Precision.HIGHEST
    lanes = lax.axis_size("ctx")
    block = signal.shape[1]
    piece = block // lanes
    total_len = 2 * lanes * block
    mine = lax.axis_index("ctx")
    order = jnp.arange(2 * lanes, dtype=jnp.int32)
    owner = order // 2
    parity = order % 2
    freq_rows = jnp.where(
        owner == 0, parity * lanes, jnp.where(parity == 0, owner, 2 * lanes - owner)
    )
    own_rows = lax.dynamic_slice_in_dim(freq_rows, 2 * mine, 2)
    sources = jnp.arange(lanes, dtype=jnp.int32)
    cross = dft_table(sources, freq_rows, 2 * lanes, -1.0)
    column_pos = mine * piece + jnp.arange(piece, dtype=jnp.int32)
    twist_c, twist_s = phase(freq_rows[:, None] * column_pos[None, :], total_len, -1.0)
    columns = to_columns(jnp.stack([signal, filters])[:, :, None, :])
    spec = jnp.einsum("scaj,qar->qscrj", columns, cross[0], precision=highest)
    spec = twisted(spec, twist_c, twist_s)
    width_dev = spec.shape[2]
    arrived = to_rows(spec.reshape((4, width_dev) + spec.shape[3:]))
    arrived = arrived.reshape((2, 2, width_dev) + arrived.shape[2:])
    freq = local_transform(arrived, -1.0)
    prod = complex_times(freq[:, 0], freq[:, 1])
    back = local_transform(prod, 1.0)
    full_pos = jnp.arange(block, dtype=jnp.int32)
    turn_c, turn_s = phase(own_rows[:, None] * full_pos[None, :], total_len, 1.0)
    back = twisted(back, turn_c, turn_s)
    spread = to_columns(back)
    merge = dft_table(freq_rows, sources, 2 * lanes, 1.0)
    partial_out = jnp.einsum("pcrj,pra->caj", spread, merge[:, 0], precision=highest)
    landed = to_rows(partial_out[None])
    return landed[0, :, 0, :] / total_len


def local(qkv, conv_taps, filters, skip):
    reach = conv_taps.shape[2] - 1
    grouped = lax.all_to_all(qkv, "ch", split_axis=1, concat_axis=2, tiled=True)
    earlier = from_behind(grouped[:, :, -reach:], "ctx", 1)
    width_dev = grouped.shape[1]
    taps_mine = lax.dynamic_slice_in_dim(conv_taps, lax.axis_index("ch") * width_dev, width_dev, 1)
    query, gated = featurize(grouped, earlier, taps_mine)
    signal = gated.astype(jnp.float32)
    long_conv = spread_conv(signal, filters)
    mixed = query.astype(jnp.float32) * (long_conv + skip[:, None] * signal)
    return mixed.astype(jnp.bfloat16)


def solution(mesh):
    lanes, groups = mesh.shape["ctx"], mesh.shape["ch"]

    def body(qkv, conv_taps, filters, skip):
        chans = qkv.shape[1] // (lanes * groups)
        fits = chans % 16 == 0 and (lanes * groups) % 8 == 0 and qkv.shape[2] % 128 == 0
        if fits:
            return fused_local(lanes, groups, qkv, conv_taps, filters, skip)
        return local(qkv, conv_taps, filters, skip)

    return jax.shard_map(
        body,
        mesh=mesh,
        in_specs=(P(None, None, ("ctx", "ch")), P(), P("ch", "ctx"), P("ch")),
        out_specs=P("ch", "ctx"),
        check_vma=False,
    )
```

```python
import functools
import math

import jax
import jax.numpy as jnp
import ml_dtypes
import numpy as np
from jax import lax
from jax.experimental import pallas as pl
from jax.experimental.pallas import tpu as pltpu
from jax.sharding import PartitionSpec as P

MESH = pl.DeviceIdType.MESH
F32 = jnp.float32
BF16 = jnp.bfloat16


def tables(devices, width, chans):
    total = 2 * devices * width
    a = np.arange(devices)
    k1 = np.arange(devices) + 0.5
    eye = np.eye(chans)
    angle = 2 * np.pi * np.outer(k1, a) / (2 * devices)
    forward = np.concatenate([np.kron(np.cos(angle), eye), np.kron(-np.sin(angle), eye)], 0)
    inverse = np.concatenate([np.kron(np.cos(angle.T), eye), np.kron(-np.sin(angle.T), eye)], 1)
    inverse = inverse * (2.0 / total)
    b = np.arange(width)
    turn = 2 * np.pi * np.outer(k1, b) / total
    twist = np.stack([np.cos(turn), np.sin(turn)])
    inner = 2 * np.pi * (np.outer(b, b) % width) / width
    cos, sin = np.cos(inner), np.sin(inner)
    wide = np.stack(
        [np.block([[cos, -sin], [sin, cos]]), np.block([[cos, sin], [-sin, cos]])]
    )
    low = lambda x: jnp.asarray(x.astype(ml_dtypes.bfloat16))
    return (
        low(forward),
        low(inverse),
        low(wide),
        jnp.asarray(twist.astype(np.float32)[:, :, None, :]),
    )


def kernel(
    lanes, groups, reach,
    qkv, taps, filters, skip, fwd_hbm, inv_hbm, wide_hbm, twist_hbm,
    out,
    qin, fraw, tapv, fwd, inv, wide, twist,
    halo_out, halo_in, tapc, tapb, skipb,
    fsend, fbuf, gsend, gbuf, qland, hspec, vbuf, mbuf, landed,
    load_sem, own_sem, send_sem, recv_sem,
):
    devices = lanes * groups
    chans, width = fbuf.shape[1], fbuf.shape[2]
    channels = qin.shape[1]
    mine = lax.axis_index("ctx")
    side = lax.axis_index("ch")
    me = mine * groups + side
    per_side = lanes * chans

    def side_rows(i):
        return pl.ds(pl.multiple_of(i * chans, chans), chans)

    loads = [
        pltpu.make_async_copy(src, dst, load_sem.at[n])
        for n, (src, dst) in enumerate(
            [
                (qkv, qin), (filters, fraw), (taps, tapv), (fwd_hbm, fwd),
                (wide_hbm, wide), (twist_hbm, twist), (inv_hbm, inv),
            ]
        )
    ]
    for load in loads:
        load.start()

    barrier = pltpu.get_barrier_semaphore()

    def greet(d, carry):
        t = lax.rem(me + d, devices)
        pl.semaphore_signal(
            barrier, inc=1, device_id=(t // groups, t % groups), device_id_type=MESH
        )
        return carry

    lax.fori_loop(1, devices, greet, 0)

    keep = 8
    parts = width // keep
    prows = channels // parts
    lane = lax.broadcasted_iota(jnp.int32, (prows, width), 1)
    loads[0].wait()
    for s in range(3):
        packed = jnp.zeros((prows, width), F32)
        for g in range(parts):
            rows = qin[s, g * prows : (g + 1) * prows].astype(F32)
            moved = pltpu.roll(rows, (keep * (g + 1)) % width, 1)
            packed = jnp.where((lane >= keep * g) & (lane < keep * (g + 1)), moved, packed)
        halo_out[s] = packed.astype(BF16)
    loads[1].wait()
    for g in range(groups):
        fsend[g] = fraw[:, g * width : (g + 1) * width].astype(BF16)

    pl.semaphore_wait(barrier, devices - 1)

    after, before = me + 1, me - 1

    def halo_copy(t):
        return pltpu.make_async_remote_copy(
            src_ref=halo_out, dst_ref=halo_in,
            send_sem=send_sem.at[0], recv_sem=recv_sem.at[0],
            device_id=(t // groups, t % groups), device_id_type=MESH,
        )

    @pl.when(me < devices - 1)
    def _():
        halo_copy(after).start()

    def send_filters(d, carry):
        i = lax.rem(mine + d, lanes)
        pltpu.make_async_remote_copy(
            src_ref=fsend.at[:, side_rows(i)],
            dst_ref=fbuf.at[pl.ds(mine * groups, groups)],
            send_sem=send_sem.at[1], recv_sem=recv_sem.at[1],
            device_id=(i, side), device_id_type=MESH,
        ).start()
        return carry

    lax.fori_loop(1, lanes, send_filters, 0)
    own_f = pltpu.make_async_copy(
        fsend.at[:, side_rows(mine)], fbuf.at[pl.ds(mine * groups, groups)], own_sem.at[0]
    )
    own_f.start()

    loads[2].wait()
    for s in range(3):
        wide_taps = jnp.concatenate(
            [tapv[s], jnp.zeros((width - reach - 1, channels), F32)], axis=0
        )
        tapc[s] = wide_taps.T

    @pl.loop(0, parts)
    def _(g):
        rows = pl.ds(pl.multiple_of(g * prows, prows), prows)
        for s in range(3):
            columns = tapc[s, rows]
            for i in range(reach + 1):
                tapb[s, i, rows] = jnp.broadcast_to(columns[:, i : i + 1], (prows, width))

    pick = lax.broadcasted_iota(jnp.int32, (chans, per_side), 1) == (
        mine * chans + lax.broadcasted_iota(jnp.int32, (chans, per_side), 0)
    )
    column = jnp.sum(jnp.where(pick, skip[...], 0.0), axis=1, keepdims=True)
    skipb[...] = jnp.broadcast_to(column, (chans, width))

    @pl.when(me > 0)
    def _():
        halo_copy(before).wait_recv()

    @pl.when(me == 0)
    def _():
        halo_in[...] = jnp.zeros_like(halo_in)

    def feature(stream, g):
        rows = pl.ds(pl.multiple_of(g * prows, prows), prows)
        cur = qin[stream, rows].astype(F32)
        prev = pltpu.roll(halo_in[stream].astype(F32), width - keep - keep * g, 1)
        acc = tapb[stream, 0, rows] * cur
        for i in range(1, reach + 1):
            moved = pltpu.roll(jnp.where(lane >= width - i, prev, cur), i, 1)
            acc = acc + tapb[stream, i, rows] * moved
        return acc

    fold = prows // chans
    side_parts = per_side // prows

    @pl.loop(0, parts)
    def _(n):
        g = lax.rem(n + me // fold, parts)
        gate = (feature(1, g) * feature(2, g)).astype(BF16)
        gsend[pl.ds(pl.multiple_of(g * prows, prows), prows)] = gate
        j = g // side_parts
        for f in range(fold):
            i = (g % side_parts) * fold + f
            src = gsend.at[pl.ds(pl.multiple_of(g * prows + f * chans, chans), chans)]
            own = jnp.logical_and(i == mine, j == side)

            @pl.when(own)
            def _():
                pltpu.make_async_copy(src, gbuf.at[me], own_sem.at[1]).start()

            @pl.when(jnp.logical_not(own))
            def _():
                pltpu.make_async_remote_copy(
                    src_ref=src, dst_ref=gbuf.at[me],
                    send_sem=send_sem.at[2], recv_sem=recv_sem.at[2],
                    device_id=(i, j), device_id_type=MESH,
                ).start()

    for j in range(groups):

        @pl.loop(0, side_parts)
        def _(n):
            rows = pl.ds(pl.multiple_of(n * prows, prows), prows)
            mbuf[j, rows] = feature(0, j * side_parts + n).astype(BF16)

    def send_query(d, carry):
        j = lax.rem(side + d, groups)
        pltpu.make_async_remote_copy(
            src_ref=mbuf.at[j], dst_ref=qland.at[side],
            send_sem=send_sem.at[3], recv_sem=recv_sem.at[3],
            device_id=(mine, j), device_id_type=MESH,
        ).start()
        return carry

    lax.fori_loop(1, groups, send_query, 0)
    own_q = pltpu.make_async_copy(mbuf.at[side], qland.at[side], own_sem.at[2])
    own_q.start()

    step = 8
    block = step * chans
    half = devices * chans

    def dot(left, right):
        return jnp.dot(left, right, preferred_element_type=F32)

    def forward(signal, r0, k0):
        real = dot(fwd[pl.ds(r0, block), :], signal).reshape(step, chans, width)
        imag = dot(fwd[pl.ds(half + r0, block), :], signal).reshape(step, chans, width)
        cos, sin = twist[0, pl.ds(k0, step)], twist[1, pl.ds(k0, step)]
        turned = jnp.concatenate(
            [
                (real * cos + imag * sin).astype(BF16).reshape(block, width),
                (imag * cos - real * sin).astype(BF16).reshape(block, width),
            ],
            axis=1,
        )
        return dot(turned, wide[0])

    for load in loads[3:]:
        load.wait()
    own_f.wait()
    got_f = fbuf.at[pl.ds(0, devices - groups)]
    pltpu.make_async_copy(got_f, got_f, recv_sem.at[1]).wait()

    @pl.loop(0, devices // step)
    def _(n):
        r0 = pl.multiple_of(n * block, block)
        hspec[pl.ds(r0, block), :] = forward(fbuf[...].reshape(half, width), r0, n * step)

    gated = gbuf.at[pl.ds(0, devices - 1)]
    pltpu.make_async_copy(gsend.at[pl.ds(0, chans)], gbuf.at[me], own_sem.at[1]).wait()
    pltpu.make_async_copy(gated, gated, recv_sem.at[2]).wait()

    @pl.loop(0, devices // step)
    def _(n):
        r0 = pl.multiple_of(n * block, block)
        spec = forward(gbuf[...].reshape(half, width), r0, n * step)
        filt = hspec[pl.ds(r0, block), :]
        sr, si = spec[:, :width], spec[:, width:]
        fr, fi = filt[:, :width], filt[:, width:]
        prod = jnp.concatenate(
            [(sr * fr - si * fi).astype(BF16), (sr * fi + si * fr).astype(BF16)], axis=1
        )
        back = dot(prod, wide[1])
        br = back[:, :width].reshape(step, chans, width)
        bi = back[:, width:].reshape(step, chans, width)
        cos, sin = twist[0, pl.ds(n * step, step)], twist[1, pl.ds(n * step, step)]
        vbuf[pl.ds(r0, block), :] = (br * cos - bi * sin).astype(BF16).reshape(block, width)
        vbuf[pl.ds(half + r0, block), :] = (
            (br * sin + bi * cos).astype(BF16).reshape(block, width)
        )

    fstep = 4
    pieces = devices // fstep
    ahead = fstep // groups

    @pl.loop(0, pieces)
    def _(n):
        m = lax.rem(n + mine // ahead, pieces)
        a0 = m * fstep
        rows = pl.ds(pl.multiple_of(a0 * chans, fstep * chans), fstep * chans)
        conv = dot(inv[rows, :], vbuf[...]).reshape(fstep, chans, width)
        signal = gbuf[pl.ds(a0, fstep)].astype(F32)
        gsend2 = (conv + skipb[...] * signal).astype(BF16)
        fbuf[pl.ds(a0, fstep)] = gsend2
        for f in range(ahead):
            i = m * ahead + f
            src = fbuf.at[pl.ds(i * groups, groups)]

            @pl.when(i == mine)
            def _():
                pltpu.make_async_copy(
                    src, landed.at[:, side_rows(mine)], own_sem.at[3]
                ).start()

            @pl.when(i != mine)
            def _():
                pltpu.make_async_remote_copy(
                    src_ref=src, dst_ref=landed.at[:, side_rows(mine)],
                    send_sem=send_sem.at[4], recv_sem=recv_sem.at[4],
                    device_id=(i, side), device_id_type=MESH,
                ).start()

    @pl.when(me < devices - 1)
    def _():
        halo_copy(after).wait_send()

    sent_f = fbuf.at[pl.ds(0, devices - groups)]
    pltpu.make_async_copy(sent_f, sent_f, send_sem.at[1]).wait()
    pltpu.make_async_copy(gated, gated, send_sem.at[2]).wait()
    others = qland.at[pl.ds(0, groups - 1)]
    pltpu.make_async_copy(others, others, send_sem.at[3]).wait()
    pltpu.make_async_copy(others, others, recv_sem.at[3]).wait()
    own_q.wait()
    pltpu.make_async_copy(sent_f, sent_f, send_sem.at[4]).wait()
    pltpu.make_async_copy(
        fbuf.at[pl.ds(0, groups)], landed.at[:, pl.ds(0, chans)], own_sem.at[3]
    ).wait()
    pltpu.make_async_copy(sent_f, sent_f, recv_sem.at[4]).wait()
    for g in range(groups):
        out[:, g * width : (g + 1) * width] = (
            qland[g].astype(F32) * landed[g].astype(F32)
        ).astype(BF16)


def fused_local(lanes, groups, qkv, conv_taps, filters, skip):
    devices = lanes * groups
    channels, width = qkv.shape[1], qkv.shape[2]
    chans = channels // devices
    count = conv_taps.shape[2]
    fwd, inv, wide, twist = tables(devices, width, chans)
    hbm = pl.BlockSpec(memory_space=pltpu.HBM)
    vmem = pl.BlockSpec(memory_space=pltpu.VMEM)
    per_side = lanes * chans
    halo = (3, channels * 8 // width, width)
    return pl.pallas_call(
        functools.partial(kernel, lanes, groups, count - 1),
        out_shape=jax.ShapeDtypeStruct((per_side, groups * width), BF16),
        in_specs=[hbm, hbm, hbm, vmem] + [hbm] * 4,
        out_specs=vmem,
        scratch_shapes=[
            pltpu.VMEM(qkv.shape, BF16),
            pltpu.VMEM(filters.shape, F32),
            pltpu.VMEM((3, count, channels), F32),
            pltpu.VMEM(fwd.shape, BF16),
            pltpu.VMEM(inv.shape, BF16),
            pltpu.VMEM(wide.shape, BF16),
            pltpu.VMEM(twist.shape, F32),
            pltpu.VMEM(halo, BF16),
            pltpu.VMEM(halo, BF16),
            pltpu.VMEM((3, channels, width), F32),
            pltpu.VMEM((3, count, channels, width), F32),
            pltpu.VMEM((chans, width), F32),
            pltpu.VMEM((groups, per_side, width), BF16),
            pltpu.VMEM((devices, chans, width), BF16),
            pltpu.VMEM((channels, width), BF16),
            pltpu.VMEM((devices, chans, width), BF16),
            pltpu.VMEM((groups, per_side, width), BF16),
            pltpu.VMEM((channels, 2 * width), F32),
            pltpu.VMEM((2 * channels, width), BF16),
            pltpu.VMEM((groups, per_side, width), BF16),
            pltpu.VMEM((groups, per_side, width), BF16),
            pltpu.SemaphoreType.DMA((7,)),
            pltpu.SemaphoreType.DMA((4,)),
            pltpu.SemaphoreType.DMA((5,)),
            pltpu.SemaphoreType.DMA((5,)),
        ],
        compiler_params=pltpu.CompilerParams(
            collective_id=0, has_side_effects=True, vmem_limit_bytes=60 * 1024 * 1024
        ),
    )(qkv, conv_taps.transpose(0, 2, 1), filters, skip.reshape(1, -1), fwd, inv, wide, twist)


def from_behind(shard, axis, by):
    length = lax.axis_size(axis)
    pairs = [(i, i + by) for i in range(length) if 0 <= i + by < length]
    return lax.ppermute(shard, axis, pairs)


def featurize(block, earlier, taps):
    reach = taps.shape[2] - 1
    length = block.shape[2]
    joined = jnp.concatenate([earlier, block], axis=2).astype(jnp.float32)
    total = jnp.zeros(block.shape, jnp.float32)
    for offset in range(taps.shape[2]):
        total = (
            total
            + taps[:, :, offset : offset + 1]
            * joined[:, :, reach - offset : reach - offset + length]
        )
    query = lax.optimization_barrier(total[0].astype(jnp.bfloat16))
    gated = lax.optimization_barrier((total[1] * total[2]).astype(jnp.bfloat16))
    return (query, gated)


def phase(product, modulus, sign):
    angle = sign * 2.0 * math.pi / modulus * (product % modulus).astype(jnp.float32)
    return (jnp.cos(angle), jnp.sin(angle))


def dft_table(index_in, index_out, modulus, sign):
    cosine, sine = phase(index_in[:, None] * index_out[None, :], modulus, sign)
    return jnp.stack([jnp.stack([cosine, sine]), jnp.stack([-sine, cosine])])


def complex_times(left, right):
    return jnp.stack(
        [left[0] * right[0] - left[1] * right[1], left[0] * right[1] + left[1] * right[0]]
    )


def twisted(values, cosine, sine):
    return jnp.stack([values[0] * cosine - values[1] * sine, values[0] * sine + values[1] * cosine])


def local_transform(values, sign):
    highest = lax.Precision.HIGHEST
    length = values.shape[-1]
    first = max((d for d in range(1, math.isqrt(length) + 1) if length % d == 0))
    second = length // first
    lead = values.shape[:-1]
    shaped = values.reshape(lead + (first, second))
    index_a = jnp.arange(first, dtype=jnp.int32)
    index_b = jnp.arange(second, dtype=jnp.int32)
    outer = dft_table(index_a, index_a, first, sign)
    part = jnp.einsum("p...ab,pqak->q...kb", shaped, outer, precision=highest)
    twist_c, twist_s = phase(index_a[:, None] * index_b[None, :], length, sign)
    part = twisted(part, twist_c, twist_s)
    inner = dft_table(index_b, index_b, second, sign)
    result = jnp.einsum("p...kb,pqbm->q...mk", part, inner, precision=highest)
    return result.reshape(lead + (length,))


def to_columns(values):
    return lax.all_to_all(
        values.astype(jnp.bfloat16), "ctx", split_axis=3, concat_axis=2, tiled=True
    ).astype(values.dtype)


def to_rows(values):
    return lax.all_to_all(
        values.astype(jnp.bfloat16), "ctx", split_axis=2, concat_axis=3, tiled=True
    ).astype(values.dtype)


def spread_conv(signal, filters):
    highest = lax.Precision.HIGHEST
    lanes = lax.axis_size("ctx")
    block = signal.shape[1]
    piece = block // lanes
    total_len = 2 * lanes * block
    mine = lax.axis_index("ctx")
    order = jnp.arange(2 * lanes, dtype=jnp.int32)
    owner = order // 2
    parity = order % 2
    freq_rows = jnp.where(
        owner == 0, parity * lanes, jnp.where(parity == 0, owner, 2 * lanes - owner)
    )
    own_rows = lax.dynamic_slice_in_dim(freq_rows, 2 * mine, 2)
    sources = jnp.arange(lanes, dtype=jnp.int32)
    cross = dft_table(sources, freq_rows, 2 * lanes, -1.0)
    column_pos = mine * piece + jnp.arange(piece, dtype=jnp.int32)
    twist_c, twist_s = phase(freq_rows[:, None] * column_pos[None, :], total_len, -1.0)
    columns = to_columns(jnp.stack([signal, filters])[:, :, None, :])
    spec = jnp.einsum("scaj,qar->qscrj", columns, cross[0], precision=highest)
    spec = twisted(spec, twist_c, twist_s)
    width_dev = spec.shape[2]
    arrived = to_rows(spec.reshape((4, width_dev) + spec.shape[3:]))
    arrived = arrived.reshape((2, 2, width_dev) + arrived.shape[2:])
    freq = local_transform(arrived, -1.0)
    prod = complex_times(freq[:, 0], freq[:, 1])
    back = local_transform(prod, 1.0)
    full_pos = jnp.arange(block, dtype=jnp.int32)
    turn_c, turn_s = phase(own_rows[:, None] * full_pos[None, :], total_len, 1.0)
    back = twisted(back, turn_c, turn_s)
    spread = to_columns(back)
    merge = dft_table(freq_rows, sources, 2 * lanes, 1.0)
    partial_out = jnp.einsum("pcrj,pra->caj", spread, merge[:, 0], precision=highest)
    landed = to_rows(partial_out[None])
    return landed[0, :, 0, :] / total_len


def local(qkv, conv_taps, filters, skip):
    reach = conv_taps.shape[2] - 1
    grouped = lax.all_to_all(qkv, "ch", split_axis=1, concat_axis=2, tiled=True)
    earlier = from_behind(grouped[:, :, -reach:], "ctx", 1)
    width_dev = grouped.shape[1]
    taps_mine = lax.dynamic_slice_in_dim(conv_taps, lax.axis_index("ch") * width_dev, width_dev, 1)
    query, gated = featurize(grouped, earlier, taps_mine)
    signal = gated.astype(jnp.float32)
    long_conv = spread_conv(signal, filters)
    mixed = query.astype(jnp.float32) * (long_conv + skip[:, None] * signal)
    return mixed.astype(jnp.bfloat16)


def solution(mesh):
    lanes, groups = mesh.shape["ctx"], mesh.shape["ch"]

    def body(qkv, conv_taps, filters, skip):
        chans = qkv.shape[1] // (lanes * groups)
        fits = (
            chans % 16 == 0
            and qkv.shape[2] == 128
            and (qkv.shape[1] // 16) % chans == 0
            and (lanes * chans) % (qkv.shape[1] // 16) == 0
            and (lanes * groups) % 8 == 0
            and 4 % groups == 0
            and conv_taps.shape[2] <= 8
        )
        if fits:
            return fused_local(lanes, groups, qkv, conv_taps, filters, skip)
        return local(qkv, conv_taps, filters, skip)

    return jax.shard_map(
        body,
        mesh=mesh,
        in_specs=(P(None, None, ("ctx", "ch")), P(), P("ch", "ctx"), P("ch")),
        out_specs=P("ch", "ctx"),
        check_vma=False,
    )
```

```python
import functools
import math

import jax
import jax.numpy as jnp
import ml_dtypes
import numpy as np
from jax import lax
from jax.experimental import pallas as pl
from jax.experimental.pallas import tpu as pltpu
from jax.sharding import PartitionSpec as P

MESH = pl.DeviceIdType.MESH
F32 = jnp.float32
BF16 = jnp.bfloat16


def tables(devices, width):
    total = 2 * devices * width
    a = np.arange(devices)
    k1 = np.arange(devices) + 0.5
    angle = 2 * np.pi * np.outer(k1, a) / (2 * devices)
    forward = np.concatenate([np.cos(angle), -np.sin(angle)], 0)
    inverse = np.concatenate([np.cos(angle.T), -np.sin(angle.T)], 1) * (2.0 / total)
    b = np.arange(width)
    turn = 2 * np.pi * np.outer(k1, b) / total
    twist = np.stack([np.cos(turn), np.sin(turn)])
    inner = 2 * np.pi * (np.outer(b, b) % width) / width
    cos, sin = np.cos(inner), np.sin(inner)
    wide = np.stack(
        [np.block([[cos, -sin], [sin, cos]]), np.block([[cos, sin], [-sin, cos]])]
    )
    low = lambda x: jnp.asarray(x.astype(ml_dtypes.bfloat16))
    return low(forward), low(inverse), low(wide), jnp.asarray(twist.astype(np.float32))


def kernel(
    lanes, groups, reach,
    qkv, taps, filters, skip, fwd_hbm, inv_hbm, wide_hbm, twist_hbm,
    out,
    qin, fraw, tapv, skipv, fwd, inv, wide, twist,
    halo_out, halo_in, tapc, tapb, skipb,
    fsend, fbuf, gsend, gbuf, qland, hspec, spread, mbuf, landed,
    load_sem, own_sem, send_sem, recv_sem,
):
    devices = lanes * groups
    chans, width = fbuf.shape[1], fbuf.shape[2]
    channels = qin.shape[1]
    mine = lax.axis_index("ctx")
    side = lax.axis_index("ch")
    me = mine * groups + side
    per_side = lanes * chans

    def side_rows(i):
        return pl.ds(pl.multiple_of(i * chans, chans), chans)

    loads = [
        pltpu.make_async_copy(src, dst, load_sem.at[n])
        for n, (src, dst) in enumerate(
            [
                (qkv, qin), (filters, fraw), (taps, tapv), (skip, skipv), (fwd_hbm, fwd),
                (wide_hbm, wide), (twist_hbm, twist), (inv_hbm, inv),
            ]
        )
    ]
    for load in loads:
        load.start()

    barrier = pltpu.get_barrier_semaphore()

    def greet(d, carry):
        t = lax.rem(me + d, devices)
        pl.semaphore_signal(
            barrier, inc=1, device_id=(t // groups, t % groups), device_id_type=MESH
        )
        return carry

    lax.fori_loop(1, devices, greet, 0)

    keep = 8
    parts = width // keep
    prows = channels // parts
    lane = lax.broadcasted_iota(jnp.int32, (prows, width), 1)
    loads[0].wait()
    for s in range(3):
        packed = jnp.zeros((prows, width), F32)
        for g in range(parts):
            rows = qin[s, g * prows : (g + 1) * prows].astype(F32)
            moved = pltpu.roll(rows, (keep * (g + 1)) % width, 1)
            packed = jnp.where((lane >= keep * g) & (lane < keep * (g + 1)), moved, packed)
        halo_out[s] = packed.astype(BF16)
    loads[1].wait()
    for g in range(groups):
        fsend[g] = fraw[:, g * width : (g + 1) * width].astype(BF16)

    pl.semaphore_wait(barrier, devices - 1)

    after, before = me + 1, me - 1

    def halo_copy(t):
        return pltpu.make_async_remote_copy(
            src_ref=halo_out, dst_ref=halo_in,
            send_sem=send_sem.at[0], recv_sem=recv_sem.at[0],
            device_id=(t // groups, t % groups), device_id_type=MESH,
        )

    @pl.when(me < devices - 1)
    def _():
        halo_copy(after).start()

    def send_filters(d, carry):
        i = lax.rem(mine + d, lanes)
        pltpu.make_async_remote_copy(
            src_ref=fsend.at[:, side_rows(i)],
            dst_ref=fbuf.at[pl.ds(mine * groups, groups)],
            send_sem=send_sem.at[1], recv_sem=recv_sem.at[1],
            device_id=(i, side), device_id_type=MESH,
        ).start()
        return carry

    lax.fori_loop(1, lanes, send_filters, 0)
    own_f = pltpu.make_async_copy(
        fsend.at[:, side_rows(mine)], fbuf.at[pl.ds(mine * groups, groups)], own_sem.at[0]
    )
    own_f.start()

    loads[2].wait()
    for s in range(3):
        wide_taps = jnp.concatenate(
            [tapv[s], jnp.zeros((width - reach - 1, channels), F32)], axis=0
        )
        tapc[s] = wide_taps.T

    @pl.loop(0, parts)
    def _(g):
        rows = pl.ds(pl.multiple_of(g * prows, prows), prows)
        for s in range(3):
            columns = tapc[s, rows]
            for i in range(reach + 1):
                tapb[s, i, rows] = jnp.broadcast_to(columns[:, i : i + 1], (prows, width))

    pick = lax.broadcasted_iota(jnp.int32, (chans, per_side), 1) == (
        mine * chans + lax.broadcasted_iota(jnp.int32, (chans, per_side), 0)
    )
    loads[3].wait()
    column = jnp.sum(jnp.where(pick, skipv[...], 0.0), axis=1, keepdims=True)
    skipb[...] = jnp.broadcast_to(column, (chans, width))

    @pl.when(me > 0)
    def _():
        halo_copy(before).wait_recv()

    @pl.when(me == 0)
    def _():
        halo_in[...] = jnp.zeros_like(halo_in)

    def feature(stream, g):
        rows = pl.ds(pl.multiple_of(g * prows, prows), prows)
        cur = qin[stream, rows].astype(F32)
        prev = pltpu.roll(halo_in[stream].astype(F32), width - keep - keep * g, 1)
        acc = tapb[stream, 0, rows] * cur
        for i in range(1, reach + 1):
            moved = pltpu.roll(jnp.where(lane >= width - i, prev, cur), i, 1)
            acc = acc + tapb[stream, i, rows] * moved
        return acc

    fold = prows // chans
    side_parts = per_side // prows

    @pl.loop(0, parts)
    def _(n):
        g = lax.rem(n + me // fold, parts)
        gate = (feature(1, g) * feature(2, g)).astype(BF16)
        gsend[pl.ds(pl.multiple_of(g * prows, prows), prows)] = gate
        j = g // side_parts
        for f in range(fold):
            i = (g % side_parts) * fold + f
            src = gsend.at[pl.ds(pl.multiple_of(g * prows + f * chans, chans), chans)]
            own = jnp.logical_and(i == mine, j == side)

            @pl.when(own)
            def _():
                pltpu.make_async_copy(src, gbuf.at[me], own_sem.at[1]).start()

            @pl.when(jnp.logical_not(own))
            def _():
                pltpu.make_async_remote_copy(
                    src_ref=src, dst_ref=gbuf.at[me],
                    send_sem=send_sem.at[2], recv_sem=recv_sem.at[2],
                    device_id=(i, j), device_id_type=MESH,
                ).start()

    for j in range(groups):

        @pl.loop(0, side_parts)
        def _(n):
            rows = pl.ds(pl.multiple_of(n * prows, prows), prows)
            mbuf[j, rows] = feature(0, j * side_parts + n).astype(BF16)

    def send_query(d, carry):
        j = lax.rem(side + d, groups)
        pltpu.make_async_remote_copy(
            src_ref=mbuf.at[j], dst_ref=qland.at[side],
            send_sem=send_sem.at[3], recv_sem=recv_sem.at[3],
            device_id=(mine, j), device_id_type=MESH,
        ).start()
        return carry

    lax.fori_loop(1, groups, send_query, 0)
    own_q = pltpu.make_async_copy(mbuf.at[side], qland.at[side], own_sem.at[2])
    own_q.start()

    half = devices * chans

    def dot(left, right):
        return jnp.dot(left, right, preferred_element_type=F32)

    def part(value, c):
        return value[:, c * width : (c + 1) * width]

    def forward(source):
        spread[...] = source[...].astype(F32).reshape(half, width)
        columns = jnp.concatenate(
            [
                spread[pl.ds(c, devices, stride=chans), :].astype(BF16)
                for c in range(chans)
            ],
            axis=1,
        )
        first = dot(fwd[...], columns)
        cos, sin = twist[0], twist[1]
        rows = []
        for c in range(chans):
            real, imag = part(first[:devices], c), part(first[devices:], c)
            rows.append(
                jnp.concatenate(
                    [
                        (real * cos + imag * sin).astype(BF16),
                        (imag * cos - real * sin).astype(BF16),
                    ],
                    axis=1,
                )
            )
        return dot(jnp.concatenate(rows, axis=0), wide[0])

    for load in loads[4:]:
        load.wait()
    own_f.wait()
    got_f = fbuf.at[pl.ds(0, devices - groups)]
    pltpu.make_async_copy(got_f, got_f, recv_sem.at[1]).wait()
    hspec[...] = forward(fbuf)

    gated = gbuf.at[pl.ds(0, devices - 1)]
    pltpu.make_async_copy(gsend.at[pl.ds(0, chans)], gbuf.at[me], own_sem.at[1]).wait()
    pltpu.make_async_copy(gated, gated, recv_sem.at[2]).wait()

    spec = forward(gbuf)
    sr, si = part(spec, 0), part(spec, 1)
    fr, fi = hspec[:, :width], hspec[:, width:]
    prod = jnp.concatenate(
        [(sr * fr - si * fi).astype(BF16), (sr * fi + si * fr).astype(BF16)], axis=1
    )
    back = dot(prod, wide[1])
    cos, sin = twist[0], twist[1]
    columns = []
    for c in range(chans):
        rows = back[c * devices : (c + 1) * devices]
        br, bi = part(rows, 0), part(rows, 1)
        columns.append(
            jnp.concatenate(
                [(br * cos - bi * sin).astype(BF16), (br * sin + bi * cos).astype(BF16)],
                axis=0,
            )
        )
    conv = dot(inv[...], jnp.concatenate(columns, axis=1))
    for c in range(chans):
        spread[pl.ds(c, devices, stride=chans), :] = part(conv, c)
    fbuf[...] = (
        spread[...].reshape(devices, chans, width)
        + skipb[...] * gbuf[...].astype(F32)
    ).astype(BF16)

    def send_out(d, carry):
        i = lax.rem(mine + d, lanes)
        pltpu.make_async_remote_copy(
            src_ref=fbuf.at[pl.ds(i * groups, groups)],
            dst_ref=landed.at[:, side_rows(mine)],
            send_sem=send_sem.at[4], recv_sem=recv_sem.at[4],
            device_id=(i, side), device_id_type=MESH,
        ).start()
        return carry

    lax.fori_loop(1, lanes, send_out, 0)
    own_o = pltpu.make_async_copy(
        fbuf.at[pl.ds(mine * groups, groups)], landed.at[:, side_rows(mine)], own_sem.at[3]
    )
    own_o.start()

    @pl.when(me < devices - 1)
    def _():
        halo_copy(after).wait_send()

    sent_f = fbuf.at[pl.ds(0, devices - groups)]
    pltpu.make_async_copy(sent_f, sent_f, send_sem.at[1]).wait()
    pltpu.make_async_copy(gated, gated, send_sem.at[2]).wait()
    others = qland.at[pl.ds(0, groups - 1)]
    pltpu.make_async_copy(others, others, send_sem.at[3]).wait()
    pltpu.make_async_copy(others, others, recv_sem.at[3]).wait()
    own_q.wait()
    pltpu.make_async_copy(sent_f, sent_f, send_sem.at[4]).wait()
    own_o.wait()
    pltpu.make_async_copy(sent_f, sent_f, recv_sem.at[4]).wait()
    for g in range(groups):
        out[:, g * width : (g + 1) * width] = (
            qland[g].astype(F32) * landed[g].astype(F32)
        ).astype(BF16)


def fused_local(lanes, groups, qkv, conv_taps, filters, skip):
    devices = lanes * groups
    channels, width = qkv.shape[1], qkv.shape[2]
    chans = channels // devices
    count = conv_taps.shape[2]
    fwd, inv, wide, twist = tables(devices, width)
    hbm = pl.BlockSpec(memory_space=pltpu.HBM)
    vmem = pl.BlockSpec(memory_space=pltpu.VMEM)
    per_side = lanes * chans
    halo = (3, channels * 8 // width, width)
    return pl.pallas_call(
        functools.partial(kernel, lanes, groups, count - 1),
        out_shape=jax.ShapeDtypeStruct((per_side, groups * width), BF16),
        in_specs=[hbm] * 8,
        out_specs=vmem,
        scratch_shapes=[
            pltpu.VMEM(qkv.shape, BF16),
            pltpu.VMEM(filters.shape, F32),
            pltpu.VMEM((3, count, channels), F32),
            pltpu.VMEM((1, per_side), F32),
            pltpu.VMEM(fwd.shape, BF16),
            pltpu.VMEM(inv.shape, BF16),
            pltpu.VMEM(wide.shape, BF16),
            pltpu.VMEM(twist.shape, F32),
            pltpu.VMEM(halo, BF16),
            pltpu.VMEM(halo, BF16),
            pltpu.VMEM((3, channels, width), F32),
            pltpu.VMEM((3, count, channels, width), F32),
            pltpu.VMEM((chans, width), F32),
            pltpu.VMEM((groups, per_side, width), BF16),
            pltpu.VMEM((devices, chans, width), BF16),
            pltpu.VMEM((channels, width), BF16),
            pltpu.VMEM((devices, chans, width), BF16),
            pltpu.VMEM((groups, per_side, width), BF16),
            pltpu.VMEM((channels, 2 * width), F32),
            pltpu.VMEM((channels, width), F32),
            pltpu.VMEM((groups, per_side, width), BF16),
            pltpu.VMEM((groups, per_side, width), BF16),
            pltpu.SemaphoreType.DMA((8,)),
            pltpu.SemaphoreType.DMA((4,)),
            pltpu.SemaphoreType.DMA((5,)),
            pltpu.SemaphoreType.DMA((5,)),
        ],
        compiler_params=pltpu.CompilerParams(
            collective_id=0, has_side_effects=True, vmem_limit_bytes=60 * 1024 * 1024
        ),
    )(qkv, conv_taps.transpose(0, 2, 1), filters, skip.reshape(1, -1), fwd, inv, wide, twist)


def from_behind(shard, axis, by):
    length = lax.axis_size(axis)
    pairs = [(i, i + by) for i in range(length) if 0 <= i + by < length]
    return lax.ppermute(shard, axis, pairs)


def featurize(block, earlier, taps):
    reach = taps.shape[2] - 1
    length = block.shape[2]
    joined = jnp.concatenate([earlier, block], axis=2).astype(jnp.float32)
    total = jnp.zeros(block.shape, jnp.float32)
    for offset in range(taps.shape[2]):
        total = (
            total
            + taps[:, :, offset : offset + 1]
            * joined[:, :, reach - offset : reach - offset + length]
        )
    query = lax.optimization_barrier(total[0].astype(jnp.bfloat16))
    gated = lax.optimization_barrier((total[1] * total[2]).astype(jnp.bfloat16))
    return (query, gated)


def phase(product, modulus, sign):
    angle = sign * 2.0 * math.pi / modulus * (product % modulus).astype(jnp.float32)
    return (jnp.cos(angle), jnp.sin(angle))


def dft_table(index_in, index_out, modulus, sign):
    cosine, sine = phase(index_in[:, None] * index_out[None, :], modulus, sign)
    return jnp.stack([jnp.stack([cosine, sine]), jnp.stack([-sine, cosine])])


def complex_times(left, right):
    return jnp.stack(
        [left[0] * right[0] - left[1] * right[1], left[0] * right[1] + left[1] * right[0]]
    )


def twisted(values, cosine, sine):
    return jnp.stack([values[0] * cosine - values[1] * sine, values[0] * sine + values[1] * cosine])


def local_transform(values, sign):
    highest = lax.Precision.HIGHEST
    length = values.shape[-1]
    first = max((d for d in range(1, math.isqrt(length) + 1) if length % d == 0))
    second = length // first
    lead = values.shape[:-1]
    shaped = values.reshape(lead + (first, second))
    index_a = jnp.arange(first, dtype=jnp.int32)
    index_b = jnp.arange(second, dtype=jnp.int32)
    outer = dft_table(index_a, index_a, first, sign)
    part = jnp.einsum("p...ab,pqak->q...kb", shaped, outer, precision=highest)
    twist_c, twist_s = phase(index_a[:, None] * index_b[None, :], length, sign)
    part = twisted(part, twist_c, twist_s)
    inner = dft_table(index_b, index_b, second, sign)
    result = jnp.einsum("p...kb,pqbm->q...mk", part, inner, precision=highest)
    return result.reshape(lead + (length,))


def to_columns(values):
    return lax.all_to_all(
        values.astype(jnp.bfloat16), "ctx", split_axis=3, concat_axis=2, tiled=True
    ).astype(values.dtype)


def to_rows(values):
    return lax.all_to_all(
        values.astype(jnp.bfloat16), "ctx", split_axis=2, concat_axis=3, tiled=True
    ).astype(values.dtype)


def spread_conv(signal, filters):
    highest = lax.Precision.HIGHEST
    lanes = lax.axis_size("ctx")
    block = signal.shape[1]
    piece = block // lanes
    total_len = 2 * lanes * block
    mine = lax.axis_index("ctx")
    order = jnp.arange(2 * lanes, dtype=jnp.int32)
    owner = order // 2
    parity = order % 2
    freq_rows = jnp.where(
        owner == 0, parity * lanes, jnp.where(parity == 0, owner, 2 * lanes - owner)
    )
    own_rows = lax.dynamic_slice_in_dim(freq_rows, 2 * mine, 2)
    sources = jnp.arange(lanes, dtype=jnp.int32)
    cross = dft_table(sources, freq_rows, 2 * lanes, -1.0)
    column_pos = mine * piece + jnp.arange(piece, dtype=jnp.int32)
    twist_c, twist_s = phase(freq_rows[:, None] * column_pos[None, :], total_len, -1.0)
    columns = to_columns(jnp.stack([signal, filters])[:, :, None, :])
    spec = jnp.einsum("scaj,qar->qscrj", columns, cross[0], precision=highest)
    spec = twisted(spec, twist_c, twist_s)
    width_dev = spec.shape[2]
    arrived = to_rows(spec.reshape((4, width_dev) + spec.shape[3:]))
    arrived = arrived.reshape((2, 2, width_dev) + arrived.shape[2:])
    freq = local_transform(arrived, -1.0)
    prod = complex_times(freq[:, 0], freq[:, 1])
    back = local_transform(prod, 1.0)
    full_pos = jnp.arange(block, dtype=jnp.int32)
    turn_c, turn_s = phase(own_rows[:, None] * full_pos[None, :], total_len, 1.0)
    back = twisted(back, turn_c, turn_s)
    spread = to_columns(back)
    merge = dft_table(freq_rows, sources, 2 * lanes, 1.0)
    partial_out = jnp.einsum("pcrj,pra->caj", spread, merge[:, 0], precision=highest)
    landed = to_rows(partial_out[None])
    return landed[0, :, 0, :] / total_len


def local(qkv, conv_taps, filters, skip):
    reach = conv_taps.shape[2] - 1
    grouped = lax.all_to_all(qkv, "ch", split_axis=1, concat_axis=2, tiled=True)
    earlier = from_behind(grouped[:, :, -reach:], "ctx", 1)
    width_dev = grouped.shape[1]
    taps_mine = lax.dynamic_slice_in_dim(conv_taps, lax.axis_index("ch") * width_dev, width_dev, 1)
    query, gated = featurize(grouped, earlier, taps_mine)
    signal = gated.astype(jnp.float32)
    long_conv = spread_conv(signal, filters)
    mixed = query.astype(jnp.float32) * (long_conv + skip[:, None] * signal)
    return mixed.astype(jnp.bfloat16)


def solution(mesh):
    lanes, groups = mesh.shape["ctx"], mesh.shape["ch"]

    def body(qkv, conv_taps, filters, skip):
        chans = qkv.shape[1] // (lanes * groups)
        fits = (
            chans % 16 == 0
            and qkv.shape[2] == 128
            and (qkv.shape[1] // 16) % chans == 0
            and (lanes * chans) % (qkv.shape[1] // 16) == 0
            and (lanes * groups) % 16 == 0
            and conv_taps.shape[2] <= 8
        )
        if fits:
            return fused_local(lanes, groups, qkv, conv_taps, filters, skip)
        return local(qkv, conv_taps, filters, skip)

    return jax.shard_map(
        body,
        mesh=mesh,
        in_specs=(P(None, None, ("ctx", "ch")), P(), P("ch", "ctx"), P("ch")),
        out_specs=P("ch", "ctx"),
        check_vma=False,
    )
```

```python
import functools
import math

import jax
import jax.numpy as jnp
import ml_dtypes
import numpy as np
from jax import lax
from jax.experimental import pallas as pl
from jax.experimental.pallas import tpu as pltpu
from jax.sharding import PartitionSpec as P

MESH = pl.DeviceIdType.MESH
F32 = jnp.float32
BF16 = jnp.bfloat16


def tables(devices, width):
    total = 2 * devices * width
    a = np.arange(devices)
    k1 = np.arange(devices) + 0.5
    angle = 2 * np.pi * np.outer(k1, a) / (2 * devices)
    forward = np.concatenate([np.cos(angle), -np.sin(angle)], 0)
    inverse = np.concatenate([np.cos(angle.T), -np.sin(angle.T)], 1) * (2.0 / total)
    b = np.arange(width)
    turn = 2 * np.pi * np.outer(k1, b) / total
    twist = np.stack([np.cos(turn), np.sin(turn)])
    inner = 2 * np.pi * (np.outer(b, b) % width) / width
    cos, sin = np.cos(inner), np.sin(inner)
    wide = np.stack(
        [np.block([[cos, -sin], [sin, cos]]), np.block([[cos, sin], [-sin, cos]])]
    )
    low = lambda x: jnp.asarray(x.astype(ml_dtypes.bfloat16))
    return low(forward), low(inverse), low(wide), jnp.asarray(twist.astype(np.float32))


def kernel(
    lanes, groups, reach,
    qkv, taps, filters, skip, fwd_hbm, inv_hbm, wide_hbm, twist_hbm,
    out,
    qin, fraw, tapv, skipv, fwd, inv, wide, twist,
    halo_out, halo_in, tapc, tapb, skipb,
    fsend, fbuf, gsend, gbuf, qland, hspec, spread, mbuf, landed,
    load_sem, own_sem, send_sem, recv_sem,
):
    devices = lanes * groups
    chans, width = fbuf.shape[1], fbuf.shape[2]
    channels = qin.shape[1]
    mine = lax.axis_index("ctx")
    side = lax.axis_index("ch")
    me = mine * groups + side
    per_side = lanes * chans

    def side_rows(i):
        return pl.ds(pl.multiple_of(i * chans, chans), chans)

    loads = [
        pltpu.make_async_copy(src, dst, load_sem.at[n])
        for n, (src, dst) in enumerate(
            [
                (qkv, qin), (filters, fraw), (taps, tapv), (skip, skipv), (fwd_hbm, fwd),
                (wide_hbm, wide), (twist_hbm, twist), (inv_hbm, inv),
            ]
        )
    ]
    for load in loads:
        load.start()

    barrier = pltpu.get_barrier_semaphore()

    def greet(d, carry):
        t = lax.rem(me + d, devices)
        pl.semaphore_signal(
            barrier, inc=1, device_id=(t // groups, t % groups), device_id_type=MESH
        )
        return carry

    lax.fori_loop(1, devices, greet, 0)

    keep = 8
    parts = width // keep
    prows = channels // parts
    lane = lax.broadcasted_iota(jnp.int32, (prows, width), 1)
    loads[0].wait()
    for s in range(3):
        packed = jnp.zeros((prows, width), F32)
        for g in range(parts):
            rows = qin[s, g * prows : (g + 1) * prows].astype(F32)
            moved = pltpu.roll(rows, (keep * (g + 1)) % width, 1)
            packed = jnp.where((lane >= keep * g) & (lane < keep * (g + 1)), moved, packed)
        halo_out[s] = packed.astype(BF16)
    loads[1].wait()
    for g in range(groups):
        fsend[g] = fraw[:, g * width : (g + 1) * width].astype(BF16)

    pl.semaphore_wait(barrier, devices - 1)

    after, before = me + 1, me - 1

    def halo_copy(t):
        return pltpu.make_async_remote_copy(
            src_ref=halo_out, dst_ref=halo_in,
            send_sem=send_sem.at[0], recv_sem=recv_sem.at[0],
            device_id=(t // groups, t % groups), device_id_type=MESH,
        )

    @pl.when(me < devices - 1)
    def _():
        halo_copy(after).start()

    def send_filters(d, carry):
        i = lax.rem(mine + d, lanes)
        pltpu.make_async_remote_copy(
            src_ref=fsend.at[:, side_rows(i)],
            dst_ref=fbuf.at[pl.ds(mine * groups, groups)],
            send_sem=send_sem.at[1], recv_sem=recv_sem.at[1],
            device_id=(i, side), device_id_type=MESH,
        ).start()
        return carry

    lax.fori_loop(1, lanes, send_filters, 0)
    own_f = pltpu.make_async_copy(
        fsend.at[:, side_rows(mine)], fbuf.at[pl.ds(mine * groups, groups)], own_sem.at[0]
    )
    own_f.start()

    loads[2].wait()
    for s in range(3):
        wide_taps = jnp.concatenate(
            [tapv[s], jnp.zeros((width - reach - 1, channels), F32)], axis=0
        )
        tapc[s] = wide_taps.T

    @pl.loop(0, parts)
    def _(g):
        rows = pl.ds(pl.multiple_of(g * prows, prows), prows)
        for s in range(3):
            columns = tapc[s, rows]
            for i in range(reach + 1):
                tapb[s, i, rows] = jnp.broadcast_to(columns[:, i : i + 1], (prows, width))

    pick = lax.broadcasted_iota(jnp.int32, (chans, per_side), 1) == (
        mine * chans + lax.broadcasted_iota(jnp.int32, (chans, per_side), 0)
    )
    loads[3].wait()
    column = jnp.sum(jnp.where(pick, skipv[...], 0.0), axis=1, keepdims=True)
    skipb[...] = jnp.broadcast_to(column, (chans, width))

    @pl.when(me > 0)
    def _():
        halo_copy(before).wait_recv()

    @pl.when(me == 0)
    def _():
        halo_in[...] = jnp.zeros_like(halo_in)

    def feature(stream, g):
        rows = pl.ds(pl.multiple_of(g * prows, prows), prows)
        cur = qin[stream, rows].astype(F32)
        prev = pltpu.roll(halo_in[stream].astype(F32), width - keep - keep * g, 1)
        acc = tapb[stream, 0, rows] * cur
        for i in range(1, reach + 1):
            moved = pltpu.roll(jnp.where(lane >= width - i, prev, cur), i, 1)
            acc = acc + tapb[stream, i, rows] * moved
        return acc

    fold = prows // chans
    side_parts = per_side // prows

    @pl.loop(0, parts)
    def _(n):
        g = lax.rem(n + me // fold, parts)
        gate = (feature(1, g) * feature(2, g)).astype(BF16)
        gsend[pl.ds(pl.multiple_of(g * prows, prows), prows)] = gate
        j = g // side_parts
        for f in range(fold):
            i = (g % side_parts) * fold + f
            src = gsend.at[pl.ds(pl.multiple_of(g * prows + f * chans, chans), chans)]
            own = jnp.logical_and(i == mine, j == side)

            @pl.when(own)
            def _():
                pltpu.make_async_copy(src, gbuf.at[me], own_sem.at[1]).start()

            @pl.when(jnp.logical_not(own))
            def _():
                pltpu.make_async_remote_copy(
                    src_ref=src, dst_ref=gbuf.at[me],
                    send_sem=send_sem.at[2], recv_sem=recv_sem.at[2],
                    device_id=(i, j), device_id_type=MESH,
                ).start()

    for j in range(groups):

        @pl.loop(0, side_parts)
        def _(n):
            rows = pl.ds(pl.multiple_of(n * prows, prows), prows)
            mbuf[j, rows] = feature(0, j * side_parts + n).astype(BF16)

    def send_query(d, carry):
        j = lax.rem(side + d, groups)
        pltpu.make_async_remote_copy(
            src_ref=mbuf.at[j], dst_ref=qland.at[side],
            send_sem=send_sem.at[3], recv_sem=recv_sem.at[3],
            device_id=(mine, j), device_id_type=MESH,
        ).start()
        return carry

    lax.fori_loop(1, groups, send_query, 0)
    own_q = pltpu.make_async_copy(mbuf.at[side], qland.at[side], own_sem.at[2])
    own_q.start()

    half = devices * chans

    def dot(left, right):
        return jnp.dot(left, right, preferred_element_type=F32)

    def part(value, c):
        return value[:, c * width : (c + 1) * width]

    def forward(source):
        spread[...] = source[...].astype(F32).reshape(half, width)
        columns = jnp.concatenate(
            [
                spread[pl.ds(c, devices, stride=chans), :].astype(BF16)
                for c in range(chans)
            ],
            axis=1,
        )
        first = dot(fwd[...], columns)
        cos, sin = twist[0], twist[1]
        rows = []
        for c in range(chans):
            real, imag = part(first[:devices], c), part(first[devices:], c)
            rows.append(
                jnp.concatenate(
                    [
                        (real * cos + imag * sin).astype(BF16),
                        (imag * cos - real * sin).astype(BF16),
                    ],
                    axis=1,
                )
            )
        return dot(jnp.concatenate(rows, axis=0), wide[0])

    for load in loads[4:]:
        load.wait()
    own_f.wait()
    got_f = fbuf.at[pl.ds(0, devices - groups)]
    pltpu.make_async_copy(got_f, got_f, recv_sem.at[1]).wait()
    hspec[...] = forward(fbuf)

    gated = gbuf.at[pl.ds(0, devices - 1)]
    pltpu.make_async_copy(gsend.at[pl.ds(0, chans)], gbuf.at[me], own_sem.at[1]).wait()
    pltpu.make_async_copy(gated, gated, recv_sem.at[2]).wait()

    spec = forward(gbuf)
    sr, si = part(spec, 0), part(spec, 1)
    fr, fi = hspec[:, :width], hspec[:, width:]
    prod = jnp.concatenate(
        [(sr * fr - si * fi).astype(BF16), (sr * fi + si * fr).astype(BF16)], axis=1
    )
    back = dot(prod, wide[1])
    cos, sin = twist[0], twist[1]
    columns = []
    for c in range(chans):
        rows = back[c * devices : (c + 1) * devices]
        br, bi = part(rows, 0), part(rows, 1)
        columns.append(
            jnp.concatenate(
                [(br * cos - bi * sin).astype(BF16), (br * sin + bi * cos).astype(BF16)],
                axis=0,
            )
        )
    conv = dot(inv[...], jnp.concatenate(columns, axis=1))
    for c in range(chans):
        spread[pl.ds(c, devices, stride=chans), :] = part(conv, c)
    fbuf[...] = (
        spread[...].reshape(devices, chans, width)
        + skipb[...] * gbuf[...].astype(F32)
    ).astype(BF16)

    def send_out(d, carry):
        i = lax.rem(mine + d, lanes)
        pltpu.make_async_remote_copy(
            src_ref=fbuf.at[pl.ds(i * groups, groups)],
            dst_ref=landed.at[:, side_rows(mine)],
            send_sem=send_sem.at[4], recv_sem=recv_sem.at[4],
            device_id=(i, side), device_id_type=MESH,
        ).start()
        return carry

    lax.fori_loop(1, lanes, send_out, 0)
    own_o = pltpu.make_async_copy(
        fbuf.at[pl.ds(mine * groups, groups)], landed.at[:, side_rows(mine)], own_sem.at[3]
    )
    own_o.start()

    @pl.when(me < devices - 1)
    def _():
        halo_copy(after).wait_send()

    sent_f = fbuf.at[pl.ds(0, devices - groups)]
    pltpu.make_async_copy(sent_f, sent_f, send_sem.at[1]).wait()
    pltpu.make_async_copy(gated, gated, send_sem.at[2]).wait()
    others = qland.at[pl.ds(0, groups - 1)]
    pltpu.make_async_copy(others, others, send_sem.at[3]).wait()
    pltpu.make_async_copy(others, others, recv_sem.at[3]).wait()
    own_q.wait()
    pltpu.make_async_copy(sent_f, sent_f, send_sem.at[4]).wait()
    own_o.wait()
    pltpu.make_async_copy(sent_f, sent_f, recv_sem.at[4]).wait()
    for g in range(groups):
        out[:, g * width : (g + 1) * width] = (
            qland[g].astype(F32) * landed[g].astype(F32)
        ).astype(BF16)


def fused_local(lanes, groups, qkv, conv_taps, filters, skip):
    devices = lanes * groups
    channels, width = qkv.shape[1], qkv.shape[2]
    chans = channels // devices
    count = conv_taps.shape[2]
    fwd, inv, wide, twist = tables(devices, width)
    hbm = pl.BlockSpec(memory_space=pltpu.HBM)
    vmem = pl.BlockSpec(memory_space=pltpu.VMEM)
    per_side = lanes * chans
    halo = (3, channels * 8 // width, width)
    return pl.pallas_call(
        functools.partial(kernel, lanes, groups, count - 1),
        out_shape=pltpu.VMEM((per_side, groups * width), BF16),
        in_specs=[hbm] * 8,
        out_specs=vmem,
        scratch_shapes=[
            pltpu.VMEM(qkv.shape, BF16),
            pltpu.VMEM(filters.shape, F32),
            pltpu.VMEM((3, count, channels), F32),
            pltpu.VMEM((1, per_side), F32),
            pltpu.VMEM(fwd.shape, BF16),
            pltpu.VMEM(inv.shape, BF16),
            pltpu.VMEM(wide.shape, BF16),
            pltpu.VMEM(twist.shape, F32),
            pltpu.VMEM(halo, BF16),
            pltpu.VMEM(halo, BF16),
            pltpu.VMEM((3, channels, width), F32),
            pltpu.VMEM((3, count, channels, width), F32),
            pltpu.VMEM((chans, width), F32),
            pltpu.VMEM((groups, per_side, width), BF16),
            pltpu.VMEM((devices, chans, width), BF16),
            pltpu.VMEM((channels, width), BF16),
            pltpu.VMEM((devices, chans, width), BF16),
            pltpu.VMEM((groups, per_side, width), BF16),
            pltpu.VMEM((channels, 2 * width), F32),
            pltpu.VMEM((channels, width), F32),
            pltpu.VMEM((groups, per_side, width), BF16),
            pltpu.VMEM((groups, per_side, width), BF16),
            pltpu.SemaphoreType.DMA((8,)),
            pltpu.SemaphoreType.DMA((4,)),
            pltpu.SemaphoreType.DMA((5,)),
            pltpu.SemaphoreType.DMA((5,)),
        ],
        compiler_params=pltpu.CompilerParams(
            collective_id=0, has_side_effects=True, vmem_limit_bytes=24 * 1024 * 1024
        ),
    )(
        *(
            pltpu.with_memory_space_constraint(operand, pltpu.HBM)
            for operand in (
                qkv, conv_taps.transpose(0, 2, 1), filters, skip.reshape(1, -1),
                fwd, inv, wide, twist,
            )
        )
    )


def from_behind(shard, axis, by):
    length = lax.axis_size(axis)
    pairs = [(i, i + by) for i in range(length) if 0 <= i + by < length]
    return lax.ppermute(shard, axis, pairs)


def featurize(block, earlier, taps):
    reach = taps.shape[2] - 1
    length = block.shape[2]
    joined = jnp.concatenate([earlier, block], axis=2).astype(jnp.float32)
    total = jnp.zeros(block.shape, jnp.float32)
    for offset in range(taps.shape[2]):
        total = (
            total
            + taps[:, :, offset : offset + 1]
            * joined[:, :, reach - offset : reach - offset + length]
        )
    query = lax.optimization_barrier(total[0].astype(jnp.bfloat16))
    gated = lax.optimization_barrier((total[1] * total[2]).astype(jnp.bfloat16))
    return (query, gated)


def phase(product, modulus, sign):
    angle = sign * 2.0 * math.pi / modulus * (product % modulus).astype(jnp.float32)
    return (jnp.cos(angle), jnp.sin(angle))


def dft_table(index_in, index_out, modulus, sign):
    cosine, sine = phase(index_in[:, None] * index_out[None, :], modulus, sign)
    return jnp.stack([jnp.stack([cosine, sine]), jnp.stack([-sine, cosine])])


def complex_times(left, right):
    return jnp.stack(
        [left[0] * right[0] - left[1] * right[1], left[0] * right[1] + left[1] * right[0]]
    )


def twisted(values, cosine, sine):
    return jnp.stack([values[0] * cosine - values[1] * sine, values[0] * sine + values[1] * cosine])


def local_transform(values, sign):
    highest = lax.Precision.HIGHEST
    length = values.shape[-1]
    first = max((d for d in range(1, math.isqrt(length) + 1) if length % d == 0))
    second = length // first
    lead = values.shape[:-1]
    shaped = values.reshape(lead + (first, second))
    index_a = jnp.arange(first, dtype=jnp.int32)
    index_b = jnp.arange(second, dtype=jnp.int32)
    outer = dft_table(index_a, index_a, first, sign)
    part = jnp.einsum("p...ab,pqak->q...kb", shaped, outer, precision=highest)
    twist_c, twist_s = phase(index_a[:, None] * index_b[None, :], length, sign)
    part = twisted(part, twist_c, twist_s)
    inner = dft_table(index_b, index_b, second, sign)
    result = jnp.einsum("p...kb,pqbm->q...mk", part, inner, precision=highest)
    return result.reshape(lead + (length,))


def to_columns(values):
    return lax.all_to_all(
        values.astype(jnp.bfloat16), "ctx", split_axis=3, concat_axis=2, tiled=True
    ).astype(values.dtype)


def to_rows(values):
    return lax.all_to_all(
        values.astype(jnp.bfloat16), "ctx", split_axis=2, concat_axis=3, tiled=True
    ).astype(values.dtype)


def spread_conv(signal, filters):
    highest = lax.Precision.HIGHEST
    lanes = lax.axis_size("ctx")
    block = signal.shape[1]
    piece = block // lanes
    total_len = 2 * lanes * block
    mine = lax.axis_index("ctx")
    order = jnp.arange(2 * lanes, dtype=jnp.int32)
    owner = order // 2
    parity = order % 2
    freq_rows = jnp.where(
        owner == 0, parity * lanes, jnp.where(parity == 0, owner, 2 * lanes - owner)
    )
    own_rows = lax.dynamic_slice_in_dim(freq_rows, 2 * mine, 2)
    sources = jnp.arange(lanes, dtype=jnp.int32)
    cross = dft_table(sources, freq_rows, 2 * lanes, -1.0)
    column_pos = mine * piece + jnp.arange(piece, dtype=jnp.int32)
    twist_c, twist_s = phase(freq_rows[:, None] * column_pos[None, :], total_len, -1.0)
    columns = to_columns(jnp.stack([signal, filters])[:, :, None, :])
    spec = jnp.einsum("scaj,qar->qscrj", columns, cross[0], precision=highest)
    spec = twisted(spec, twist_c, twist_s)
    width_dev = spec.shape[2]
    arrived = to_rows(spec.reshape((4, width_dev) + spec.shape[3:]))
    arrived = arrived.reshape((2, 2, width_dev) + arrived.shape[2:])
    freq = local_transform(arrived, -1.0)
    prod = complex_times(freq[:, 0], freq[:, 1])
    back = local_transform(prod, 1.0)
    full_pos = jnp.arange(block, dtype=jnp.int32)
    turn_c, turn_s = phase(own_rows[:, None] * full_pos[None, :], total_len, 1.0)
    back = twisted(back, turn_c, turn_s)
    spread = to_columns(back)
    merge = dft_table(freq_rows, sources, 2 * lanes, 1.0)
    partial_out = jnp.einsum("pcrj,pra->caj", spread, merge[:, 0], precision=highest)
    landed = to_rows(partial_out[None])
    return landed[0, :, 0, :] / total_len


def local(qkv, conv_taps, filters, skip):
    reach = conv_taps.shape[2] - 1
    grouped = lax.all_to_all(qkv, "ch", split_axis=1, concat_axis=2, tiled=True)
    earlier = from_behind(grouped[:, :, -reach:], "ctx", 1)
    width_dev = grouped.shape[1]
    taps_mine = lax.dynamic_slice_in_dim(conv_taps, lax.axis_index("ch") * width_dev, width_dev, 1)
    query, gated = featurize(grouped, earlier, taps_mine)
    signal = gated.astype(jnp.float32)
    long_conv = spread_conv(signal, filters)
    mixed = query.astype(jnp.float32) * (long_conv + skip[:, None] * signal)
    return mixed.astype(jnp.bfloat16)


def solution(mesh):
    lanes, groups = mesh.shape["ctx"], mesh.shape["ch"]

    def body(qkv, conv_taps, filters, skip):
        chans = qkv.shape[1] // (lanes * groups)
        fits = (
            chans % 16 == 0
            and qkv.shape[2] == 128
            and (qkv.shape[1] // 16) % chans == 0
            and (lanes * chans) % (qkv.shape[1] // 16) == 0
            and (lanes * groups) % 16 == 0
            and conv_taps.shape[2] <= 8
        )
        if fits:
            return fused_local(lanes, groups, qkv, conv_taps, filters, skip)
        return local(qkv, conv_taps, filters, skip)

    return jax.shard_map(
        body,
        mesh=mesh,
        in_specs=(P(None, None, ("ctx", "ch")), P(), P("ch", "ctx"), P("ch")),
        out_specs=P("ch", "ctx"),
        check_vma=False,
    )
```

```python
import functools
import math

import jax
import jax.numpy as jnp
import ml_dtypes
import numpy as np
from jax import lax
from jax.experimental import pallas as pl
from jax.experimental.pallas import tpu as pltpu
from jax.sharding import PartitionSpec as P

MESH = pl.DeviceIdType.MESH
F32 = jnp.float32
BF16 = jnp.bfloat16


def tables(devices, width):
    total = 2 * devices * width
    a = np.arange(devices)
    k1 = np.arange(devices) + 0.5
    angle = 2 * np.pi * np.outer(k1, a) / (2 * devices)
    forward = np.concatenate([np.cos(angle), -np.sin(angle)], 0)
    inverse = np.concatenate([np.cos(angle.T), -np.sin(angle.T)], 1) * (2.0 / total)
    b = np.arange(width)
    turn = 2 * np.pi * np.outer(k1, b) / total
    twist = np.stack([np.cos(turn), np.sin(turn)])
    inner = 2 * np.pi * (np.outer(b, b) % width) / width
    cos, sin = np.cos(inner), np.sin(inner)
    wide = np.stack(
        [np.block([[cos, -sin], [sin, cos]]), np.block([[cos, sin], [-sin, cos]])]
    )
    low = lambda x: jnp.asarray(x.astype(ml_dtypes.bfloat16))
    return low(forward), low(inverse), low(wide), jnp.asarray(twist.astype(np.float32))


def kernel(
    lanes, groups, reach,
    qkv, taps, filters, skip, fwd_hbm, inv_hbm, wide_hbm, twist_hbm,
    out,
    qin, fraw, tapv, skipv, fwd, inv, wide, twist,
    halo_out, halo_in, tapc, ptaps, feat, skipb,
    fsend, fbuf, gsend, gbuf, qland, hspec, spread, mbuf, landed,
    load_sem, own_sem, send_sem, recv_sem,
):
    devices = lanes * groups
    chans, width = fbuf.shape[1], fbuf.shape[2]
    channels = qin.shape[1]
    mine = lax.axis_index("ctx")
    side = lax.axis_index("ch")
    me = mine * groups + side
    per_side = lanes * chans

    def side_rows(i):
        return pl.ds(pl.multiple_of(i * chans, chans), chans)

    loads = [
        pltpu.make_async_copy(src, dst, load_sem.at[n])
        for n, (src, dst) in enumerate(
            [
                (qkv, qin), (filters, fraw), (taps, tapv), (skip, skipv), (fwd_hbm, fwd),
                (wide_hbm, wide), (twist_hbm, twist), (inv_hbm, inv),
            ]
        )
    ]
    for load in loads:
        load.start()

    barrier = pltpu.get_barrier_semaphore()

    def greet(d, carry):
        t = lax.rem(me + d, devices)
        pl.semaphore_signal(
            barrier, inc=1, device_id=(t // groups, t % groups), device_id_type=MESH
        )
        return carry

    lax.fori_loop(1, devices, greet, 0)

    keep = 8
    parts = width // keep
    prows = channels // parts
    lane = lax.broadcasted_iota(jnp.int32, (prows, width), 1)
    loads[0].wait()
    for s in range(3):
        packed = jnp.zeros((prows, width), F32)
        for g in range(parts):
            rows = qin[s, g * prows : (g + 1) * prows].astype(F32)
            moved = pltpu.roll(rows, (keep * (g + 1)) % width, 1)
            packed = jnp.where((lane >= keep * g) & (lane < keep * (g + 1)), moved, packed)
        halo_out[s] = packed.astype(BF16)
    loads[1].wait()
    for g in range(groups):
        fsend[g] = fraw[:, g * width : (g + 1) * width].astype(BF16)

    pl.semaphore_wait(barrier, devices - 1)

    after, before = me + 1, me - 1

    def halo_copy(t):
        return pltpu.make_async_remote_copy(
            src_ref=halo_out, dst_ref=halo_in,
            send_sem=send_sem.at[0], recv_sem=recv_sem.at[0],
            device_id=(t // groups, t % groups), device_id_type=MESH,
        )

    @pl.when(me < devices - 1)
    def _():
        halo_copy(after).start()

    def send_filters(d, carry):
        i = lax.rem(mine + d, lanes)
        pltpu.make_async_remote_copy(
            src_ref=fsend.at[:, side_rows(i)],
            dst_ref=fbuf.at[pl.ds(mine * groups, groups)],
            send_sem=send_sem.at[1], recv_sem=recv_sem.at[1],
            device_id=(i, side), device_id_type=MESH,
        ).start()
        return carry

    lax.fori_loop(lanes // 2, lanes, send_filters, 0)
    lax.fori_loop(1, lanes // 2, send_filters, 0)
    own_f = pltpu.make_async_copy(
        fsend.at[:, side_rows(mine)], fbuf.at[pl.ds(mine * groups, groups)], own_sem.at[0]
    )
    own_f.start()

    loads[2].wait()
    for s in range(3):
        wide_taps = jnp.concatenate(
            [tapv[s], jnp.zeros((width - reach - 1, channels), F32)], axis=0
        )
        tapc[s] = wide_taps.T

    spot = lax.rem(lane, keep)
    ptaps[...] = jnp.zeros_like(ptaps)

    @pl.loop(0, parts)
    def _(g):
        rows = pl.ds(pl.multiple_of(g * prows, prows), prows)
        here = (lane >= keep * g) & (lane < keep * (g + 1))
        for s in range(3):
            columns = tapc[s, rows]
            cur = qin[s, rows].astype(F32)
            acc = columns[:, :1] * cur
            for i in range(1, reach + 1):
                tap = jnp.broadcast_to(columns[:, i : i + 1], (prows, width))
                acc = acc + jnp.where(lane >= i, tap * pltpu.roll(cur, i, 1), 0.0)
                ptaps[s, i - 1] = jnp.where(here & (spot < i), tap, ptaps[s, i - 1])
            feat[s, rows] = acc

    pick = lax.broadcasted_iota(jnp.int32, (chans, per_side), 1) == (
        mine * chans + lax.broadcasted_iota(jnp.int32, (chans, per_side), 0)
    )
    loads[3].wait()
    column = jnp.sum(jnp.where(pick, skipv[...], 0.0), axis=1, keepdims=True)
    skipb[...] = jnp.broadcast_to(column, (chans, width))

    @pl.when(me > 0)
    def _():
        halo_copy(before).wait_recv()

    @pl.when(me == 0)
    def _():
        halo_in[...] = jnp.zeros_like(halo_in)

    added = []
    for s in range(3):
        tail = halo_in[s].astype(F32)
        total = jnp.zeros((prows, width), F32)
        for i in range(1, reach + 1):
            total = total + ptaps[s, i - 1] * pltpu.roll(tail, width - keep + i, 1)
        added.append(total)

    def feature(stream, g):
        more = pltpu.roll(added[stream], (width - keep * g) % width, 1)
        return feat[stream, g * prows : (g + 1) * prows] + jnp.where(lane < keep, more, 0.0)

    for g in range(parts):
        gsend[g * prows : (g + 1) * prows] = (feature(1, g) * feature(2, g)).astype(BF16)

    def send_gated(d, carry):
        t = lax.rem(me + d, devices)
        i, j = t // groups, t % groups
        row0 = pl.multiple_of(j * per_side + i * chans, chans)
        pltpu.make_async_remote_copy(
            src_ref=gsend.at[pl.ds(row0, chans)], dst_ref=gbuf.at[me],
            send_sem=send_sem.at[2], recv_sem=recv_sem.at[2],
            device_id=(i, j), device_id_type=MESH,
        ).start()
        return carry

    lax.fori_loop(devices // 2, devices, send_gated, 0)
    lax.fori_loop(1, devices // 2, send_gated, 0)
    own_row = pl.multiple_of(side * per_side + mine * chans, chans)
    own_g = pltpu.make_async_copy(gsend.at[pl.ds(own_row, chans)], gbuf.at[me], own_sem.at[1])
    own_g.start()

    side_parts = per_side // prows
    for g in range(parts):
        at = (g % side_parts) * prows
        mbuf[g // side_parts, at : at + prows] = feature(0, g).astype(BF16)

    def send_query(d, carry):
        j = lax.rem(side + d, groups)
        pltpu.make_async_remote_copy(
            src_ref=mbuf.at[j], dst_ref=qland.at[side],
            send_sem=send_sem.at[3], recv_sem=recv_sem.at[3],
            device_id=(mine, j), device_id_type=MESH,
        ).start()
        return carry

    lax.fori_loop(1, groups, send_query, 0)
    own_q = pltpu.make_async_copy(mbuf.at[side], qland.at[side], own_sem.at[2])
    own_q.start()

    half = devices * chans

    def dot(left, right):
        return jnp.dot(left, right, preferred_element_type=F32)

    def part(value, c):
        return value[:, c * width : (c + 1) * width]

    def forward(source):
        spread[...] = source[...].astype(F32).reshape(half, width)
        columns = jnp.concatenate(
            [
                spread[pl.ds(c, devices, stride=chans), :].astype(BF16)
                for c in range(chans)
            ],
            axis=1,
        )
        first = dot(fwd[...], columns)
        cos, sin = twist[0], twist[1]
        rows = []
        for c in range(chans):
            real, imag = part(first[:devices], c), part(first[devices:], c)
            rows.append(
                jnp.concatenate(
                    [
                        (real * cos + imag * sin).astype(BF16),
                        (imag * cos - real * sin).astype(BF16),
                    ],
                    axis=1,
                )
            )
        return dot(jnp.concatenate(rows, axis=0), wide[0])

    for load in loads[4:]:
        load.wait()
    own_f.wait()
    got_f = fbuf.at[pl.ds(0, devices - groups)]
    pltpu.make_async_copy(got_f, got_f, recv_sem.at[1]).wait()
    hspec[...] = forward(fbuf)

    gated = gbuf.at[pl.ds(0, devices - 1)]
    own_g.wait()
    pltpu.make_async_copy(gated, gated, recv_sem.at[2]).wait()

    spec = forward(gbuf)
    sr, si = part(spec, 0), part(spec, 1)
    fr, fi = hspec[:, :width], hspec[:, width:]
    prod = jnp.concatenate(
        [(sr * fr - si * fi).astype(BF16), (sr * fi + si * fr).astype(BF16)], axis=1
    )
    back = dot(prod, wide[1])
    cos, sin = twist[0], twist[1]
    columns = []
    for c in range(chans):
        rows = back[c * devices : (c + 1) * devices]
        br, bi = part(rows, 0), part(rows, 1)
        columns.append(
            jnp.concatenate(
                [(br * cos - bi * sin).astype(BF16), (br * sin + bi * cos).astype(BF16)],
                axis=0,
            )
        )
    conv = dot(inv[...], jnp.concatenate(columns, axis=1))
    for c in range(chans):
        spread[pl.ds(c, devices, stride=chans), :] = part(conv, c)
    fbuf[...] = (
        spread[...].reshape(devices, chans, width)
        + skipb[...] * gbuf[...].astype(F32)
    ).astype(BF16)

    def send_out(d, carry):
        i = lax.rem(mine + d, lanes)
        pltpu.make_async_remote_copy(
            src_ref=fbuf.at[pl.ds(i * groups, groups)],
            dst_ref=landed.at[:, side_rows(mine)],
            send_sem=send_sem.at[4], recv_sem=recv_sem.at[4],
            device_id=(i, side), device_id_type=MESH,
        ).start()
        return carry

    lax.fori_loop(lanes // 2, lanes, send_out, 0)
    lax.fori_loop(1, lanes // 2, send_out, 0)
    own_o = pltpu.make_async_copy(
        fbuf.at[pl.ds(mine * groups, groups)], landed.at[:, side_rows(mine)], own_sem.at[3]
    )
    own_o.start()

    @pl.when(me < devices - 1)
    def _():
        halo_copy(after).wait_send()

    sent_f = fbuf.at[pl.ds(0, devices - groups)]
    pltpu.make_async_copy(sent_f, sent_f, send_sem.at[1]).wait()
    pltpu.make_async_copy(gated, gated, send_sem.at[2]).wait()
    others = qland.at[pl.ds(0, groups - 1)]
    pltpu.make_async_copy(others, others, send_sem.at[3]).wait()
    pltpu.make_async_copy(others, others, recv_sem.at[3]).wait()
    own_q.wait()
    pltpu.make_async_copy(sent_f, sent_f, send_sem.at[4]).wait()
    own_o.wait()
    pltpu.make_async_copy(sent_f, sent_f, recv_sem.at[4]).wait()
    for g in range(groups):
        out[:, g * width : (g + 1) * width] = (
            qland[g].astype(F32) * landed[g].astype(F32)
        ).astype(BF16)


def fused_local(lanes, groups, qkv, conv_taps, filters, skip):
    devices = lanes * groups
    channels, width = qkv.shape[1], qkv.shape[2]
    chans = channels // devices
    count = conv_taps.shape[2]
    fwd, inv, wide, twist = tables(devices, width)
    hbm = pl.BlockSpec(memory_space=pltpu.HBM)
    vmem = pl.BlockSpec(memory_space=pltpu.VMEM)
    per_side = lanes * chans
    halo = (3, channels * 8 // width, width)
    return pl.pallas_call(
        functools.partial(kernel, lanes, groups, count - 1),
        out_shape=pltpu.VMEM((per_side, groups * width), BF16),
        in_specs=[hbm] * 8,
        out_specs=vmem,
        scratch_shapes=[
            pltpu.VMEM(qkv.shape, BF16),
            pltpu.VMEM(filters.shape, F32),
            pltpu.VMEM((3, count, channels), F32),
            pltpu.VMEM((1, per_side), F32),
            pltpu.VMEM(fwd.shape, BF16),
            pltpu.VMEM(inv.shape, BF16),
            pltpu.VMEM(wide.shape, BF16),
            pltpu.VMEM(twist.shape, F32),
            pltpu.VMEM(halo, BF16),
            pltpu.VMEM(halo, BF16),
            pltpu.VMEM((3, channels, width), F32),
            pltpu.VMEM((3, count - 1, halo[1], width), F32),
            pltpu.VMEM((3, channels, width), F32),
            pltpu.VMEM((chans, width), F32),
            pltpu.VMEM((groups, per_side, width), BF16),
            pltpu.VMEM((devices, chans, width), BF16),
            pltpu.VMEM((channels, width), BF16),
            pltpu.VMEM((devices, chans, width), BF16),
            pltpu.VMEM((groups, per_side, width), BF16),
            pltpu.VMEM((channels, 2 * width), F32),
            pltpu.VMEM((channels, width), F32),
            pltpu.VMEM((groups, per_side, width), BF16),
            pltpu.VMEM((groups, per_side, width), BF16),
            pltpu.SemaphoreType.DMA((8,)),
            pltpu.SemaphoreType.DMA((4,)),
            pltpu.SemaphoreType.DMA((5,)),
            pltpu.SemaphoreType.DMA((5,)),
        ],
        compiler_params=pltpu.CompilerParams(
            collective_id=0, has_side_effects=True, vmem_limit_bytes=24 * 1024 * 1024
        ),
    )(
        *(
            pltpu.with_memory_space_constraint(operand, pltpu.HBM)
            for operand in (
                qkv, conv_taps.transpose(0, 2, 1), filters, skip.reshape(1, -1),
                fwd, inv, wide, twist,
            )
        )
    )


def from_behind(shard, axis, by):
    length = lax.axis_size(axis)
    pairs = [(i, i + by) for i in range(length) if 0 <= i + by < length]
    return lax.ppermute(shard, axis, pairs)


def featurize(block, earlier, taps):
    reach = taps.shape[2] - 1
    length = block.shape[2]
    joined = jnp.concatenate([earlier, block], axis=2).astype(jnp.float32)
    total = jnp.zeros(block.shape, jnp.float32)
    for offset in range(taps.shape[2]):
        total = (
            total
            + taps[:, :, offset : offset + 1]
            * joined[:, :, reach - offset : reach - offset + length]
        )
    query = lax.optimization_barrier(total[0].astype(jnp.bfloat16))
    gated = lax.optimization_barrier((total[1] * total[2]).astype(jnp.bfloat16))
    return (query, gated)


def phase(product, modulus, sign):
    angle = sign * 2.0 * math.pi / modulus * (product % modulus).astype(jnp.float32)
    return (jnp.cos(angle), jnp.sin(angle))


def dft_table(index_in, index_out, modulus, sign):
    cosine, sine = phase(index_in[:, None] * index_out[None, :], modulus, sign)
    return jnp.stack([jnp.stack([cosine, sine]), jnp.stack([-sine, cosine])])


def complex_times(left, right):
    return jnp.stack(
        [left[0] * right[0] - left[1] * right[1], left[0] * right[1] + left[1] * right[0]]
    )


def twisted(values, cosine, sine):
    return jnp.stack([values[0] * cosine - values[1] * sine, values[0] * sine + values[1] * cosine])


def local_transform(values, sign):
    highest = lax.Precision.HIGHEST
    length = values.shape[-1]
    first = max((d for d in range(1, math.isqrt(length) + 1) if length % d == 0))
    second = length // first
    lead = values.shape[:-1]
    shaped = values.reshape(lead + (first, second))
    index_a = jnp.arange(first, dtype=jnp.int32)
    index_b = jnp.arange(second, dtype=jnp.int32)
    outer = dft_table(index_a, index_a, first, sign)
    part = jnp.einsum("p...ab,pqak->q...kb", shaped, outer, precision=highest)
    twist_c, twist_s = phase(index_a[:, None] * index_b[None, :], length, sign)
    part = twisted(part, twist_c, twist_s)
    inner = dft_table(index_b, index_b, second, sign)
    result = jnp.einsum("p...kb,pqbm->q...mk", part, inner, precision=highest)
    return result.reshape(lead + (length,))


def to_columns(values):
    return lax.all_to_all(
        values.astype(jnp.bfloat16), "ctx", split_axis=3, concat_axis=2, tiled=True
    ).astype(values.dtype)


def to_rows(values):
    return lax.all_to_all(
        values.astype(jnp.bfloat16), "ctx", split_axis=2, concat_axis=3, tiled=True
    ).astype(values.dtype)


def spread_conv(signal, filters):
    highest = lax.Precision.HIGHEST
    lanes = lax.axis_size("ctx")
    block = signal.shape[1]
    piece = block // lanes
    total_len = 2 * lanes * block
    mine = lax.axis_index("ctx")
    order = jnp.arange(2 * lanes, dtype=jnp.int32)
    owner = order // 2
    parity = order % 2
    freq_rows = jnp.where(
        owner == 0, parity * lanes, jnp.where(parity == 0, owner, 2 * lanes - owner)
    )
    own_rows = lax.dynamic_slice_in_dim(freq_rows, 2 * mine, 2)
    sources = jnp.arange(lanes, dtype=jnp.int32)
    cross = dft_table(sources, freq_rows, 2 * lanes, -1.0)
    column_pos = mine * piece + jnp.arange(piece, dtype=jnp.int32)
    twist_c, twist_s = phase(freq_rows[:, None] * column_pos[None, :], total_len, -1.0)
    columns = to_columns(jnp.stack([signal, filters])[:, :, None, :])
    spec = jnp.einsum("scaj,qar->qscrj", columns, cross[0], precision=highest)
    spec = twisted(spec, twist_c, twist_s)
    width_dev = spec.shape[2]
    arrived = to_rows(spec.reshape((4, width_dev) + spec.shape[3:]))
    arrived = arrived.reshape((2, 2, width_dev) + arrived.shape[2:])
    freq = local_transform(arrived, -1.0)
    prod = complex_times(freq[:, 0], freq[:, 1])
    back = local_transform(prod, 1.0)
    full_pos = jnp.arange(block, dtype=jnp.int32)
    turn_c, turn_s = phase(own_rows[:, None] * full_pos[None, :], total_len, 1.0)
    back = twisted(back, turn_c, turn_s)
    spread = to_columns(back)
    merge = dft_table(freq_rows, sources, 2 * lanes, 1.0)
    partial_out = jnp.einsum("pcrj,pra->caj", spread, merge[:, 0], precision=highest)
    landed = to_rows(partial_out[None])
    return landed[0, :, 0, :] / total_len


def local(qkv, conv_taps, filters, skip):
    reach = conv_taps.shape[2] - 1
    grouped = lax.all_to_all(qkv, "ch", split_axis=1, concat_axis=2, tiled=True)
    earlier = from_behind(grouped[:, :, -reach:], "ctx", 1)
    width_dev = grouped.shape[1]
    taps_mine = lax.dynamic_slice_in_dim(conv_taps, lax.axis_index("ch") * width_dev, width_dev, 1)
    query, gated = featurize(grouped, earlier, taps_mine)
    signal = gated.astype(jnp.float32)
    long_conv = spread_conv(signal, filters)
    mixed = query.astype(jnp.float32) * (long_conv + skip[:, None] * signal)
    return mixed.astype(jnp.bfloat16)


def solution(mesh):
    lanes, groups = mesh.shape["ctx"], mesh.shape["ch"]

    def body(qkv, conv_taps, filters, skip):
        chans = qkv.shape[1] // (lanes * groups)
        fits = (
            chans % 16 == 0
            and qkv.shape[2] == 128
            and (qkv.shape[1] // 16) % chans == 0
            and (lanes * chans) % (qkv.shape[1] // 16) == 0
            and (lanes * groups) % 16 == 0
            and conv_taps.shape[2] <= 8
        )
        if fits:
            return fused_local(lanes, groups, qkv, conv_taps, filters, skip)
        return local(qkv, conv_taps, filters, skip)

    return jax.shard_map(
        body,
        mesh=mesh,
        in_specs=(P(None, None, ("ctx", "ch")), P(), P("ch", "ctx"), P("ch")),
        out_specs=P("ch", "ctx"),
        check_vma=False,
    )
```

```python
import functools
import math

import jax
import jax.numpy as jnp
import ml_dtypes
import numpy as np
from jax import lax
from jax.experimental import pallas as pl
from jax.experimental.pallas import tpu as pltpu
from jax.sharding import PartitionSpec as P

MESH = pl.DeviceIdType.MESH
F32 = jnp.float32
BF16 = jnp.bfloat16


def tables(devices, width):
    total = 2 * devices * width
    a = np.arange(devices)
    k1 = np.arange(devices) + 0.5
    angle = 2 * np.pi * np.outer(k1, a) / (2 * devices)
    forward = np.concatenate([np.cos(angle), -np.sin(angle)], 0)
    inverse = np.concatenate([np.cos(angle.T), -np.sin(angle.T)], 1) * (2.0 / total)
    b = np.arange(width)
    turn = 2 * np.pi * np.outer(k1, b) / total
    twist = np.stack([np.cos(turn), np.sin(turn)])
    inner = 2 * np.pi * (np.outer(b, b) % width) / width
    cos, sin = np.cos(inner), np.sin(inner)
    wide = np.stack(
        [np.block([[cos, -sin], [sin, cos]]), np.block([[cos, sin], [-sin, cos]])]
    )
    low = lambda x: jnp.asarray(x.astype(ml_dtypes.bfloat16))
    return low(forward), low(inverse), low(wide), jnp.asarray(twist.astype(np.float32))


def kernel(
    lanes, groups, reach,
    qkv, taps, filters, skip, fwd_hbm, inv_hbm, wide_hbm, twist_hbm,
    out,
    qin, fraw, tapv, skipv, fwd, inv, wide, twist,
    halo_out, halo_in, tapc, ptaps, fixes, feat, skipb,
    fsend, fbuf, gsend, gbuf, qland, hspec, spread, mbuf, landed,
    load_sem, own_sem, send_sem, recv_sem,
):
    devices = lanes * groups
    chans, width = fbuf.shape[1], fbuf.shape[2]
    channels = qin.shape[1]
    mine = lax.axis_index("ctx")
    side = lax.axis_index("ch")
    me = mine * groups + side
    per_side = lanes * chans

    def side_rows(i):
        return pl.ds(pl.multiple_of(i * chans, chans), chans)

    loads = [
        pltpu.make_async_copy(src, dst, load_sem.at[n])
        for n, (src, dst) in enumerate(
            [
                (qkv, qin), (filters, fraw), (taps, tapv), (skip, skipv), (fwd_hbm, fwd),
                (wide_hbm, wide), (twist_hbm, twist), (inv_hbm, inv),
            ]
        )
    ]
    for load in loads:
        load.start()

    barrier = pltpu.get_barrier_semaphore()

    def greet(d, carry):
        t = lax.rem(me + d, devices)
        pl.semaphore_signal(
            barrier, inc=1, device_id=(t // groups, t % groups), device_id_type=MESH
        )
        return carry

    lax.fori_loop(1, devices, greet, 0)

    keep = 8
    parts = width // keep
    prows = channels // parts
    lane = lax.broadcasted_iota(jnp.int32, (prows, width), 1)
    loads[0].wait()
    for s in range(3):
        packed = jnp.zeros((prows, width), F32)
        for g in range(parts):
            rows = qin[s, g * prows : (g + 1) * prows].astype(F32)
            moved = pltpu.roll(rows, (keep * (g + 1)) % width, 1)
            packed = jnp.where((lane >= keep * g) & (lane < keep * (g + 1)), moved, packed)
        halo_out[s] = packed.astype(BF16)
    loads[1].wait()
    for g in range(groups):
        fsend[g] = fraw[:, g * width : (g + 1) * width].astype(BF16)

    pl.semaphore_wait(barrier, devices - 1)

    after, before = me + 1, me - 1

    def halo_copy(t):
        return pltpu.make_async_remote_copy(
            src_ref=halo_out, dst_ref=halo_in,
            send_sem=send_sem.at[0], recv_sem=recv_sem.at[0],
            device_id=(t // groups, t % groups), device_id_type=MESH,
        )

    @pl.when(me < devices - 1)
    def _():
        halo_copy(after).start()

    def send_filters(d, carry):
        i = lax.rem(mine + d, lanes)
        pltpu.make_async_remote_copy(
            src_ref=fsend.at[:, side_rows(i)],
            dst_ref=fbuf.at[pl.ds(mine * groups, groups)],
            send_sem=send_sem.at[1], recv_sem=recv_sem.at[1],
            device_id=(i, side), device_id_type=MESH,
        ).start()
        return carry

    lax.fori_loop(1, lanes, send_filters, 0)
    own_f = pltpu.make_async_copy(
        fsend.at[:, side_rows(mine)], fbuf.at[pl.ds(mine * groups, groups)], own_sem.at[0]
    )
    own_f.start()

    loads[2].wait()
    for s in range(3):
        wide_taps = jnp.concatenate(
            [tapv[s], jnp.zeros((width - reach - 1, channels), F32)], axis=0
        )
        tapc[s] = wide_taps.T

    spot = lax.rem(lane, keep)
    ptaps[...] = jnp.zeros_like(ptaps)

    def partial(streams):
        @pl.loop(0, parts)
        def _(g):
            rows = pl.ds(pl.multiple_of(g * prows, prows), prows)
            here = (lane >= keep * g) & (lane < keep * (g + 1))
            for s in streams:
                columns = tapc[s, rows]
                cur = qin[s, rows].astype(F32)
                acc = columns[:, :1] * cur
                for i in range(1, reach + 1):
                    tap = jnp.broadcast_to(columns[:, i : i + 1], (prows, width))
                    acc = acc + jnp.where(lane >= i, tap * pltpu.roll(cur, i, 1), 0.0)
                    ptaps[s, i - 1] = jnp.where(here & (spot < i), tap, ptaps[s, i - 1])
                feat[s, rows] = acc

    partial((1, 2))

    pick = lax.broadcasted_iota(jnp.int32, (chans, per_side), 1) == (
        mine * chans + lax.broadcasted_iota(jnp.int32, (chans, per_side), 0)
    )
    loads[3].wait()
    column = jnp.sum(jnp.where(pick, skipv[...], 0.0), axis=1, keepdims=True)
    skipb[...] = jnp.broadcast_to(column, (chans, width))

    @pl.when(me > 0)
    def _():
        halo_copy(before).wait_recv()

    @pl.when(me == 0)
    def _():
        halo_in[...] = jnp.zeros_like(halo_in)

    def correct(s):
        tail = halo_in[s].astype(F32)
        total = jnp.zeros((prows, width), F32)
        for i in range(1, reach + 1):
            total = total + ptaps[s, i - 1] * pltpu.roll(tail, width - keep + i, 1)
        fixes[s] = total

    def feature(stream, g):
        rows = pl.ds(pl.multiple_of(g * prows, prows), prows)
        more = pltpu.roll(fixes[stream], lax.rem(width - keep * g, width), 1)
        return feat[stream, rows] + jnp.where(lane < keep, more, 0.0)

    correct(1)
    correct(2)
    fold = prows // chans
    side_parts = per_side // prows

    @pl.loop(0, parts)
    def _(n):
        g = lax.rem(n + me // fold, parts)
        gate = (feature(1, g) * feature(2, g)).astype(BF16)
        gsend[pl.ds(pl.multiple_of(g * prows, prows), prows)] = gate
        j = g // side_parts
        for f in range(fold):
            i = (g % side_parts) * fold + f
            src = gsend.at[pl.ds(pl.multiple_of(g * prows + f * chans, chans), chans)]
            own = jnp.logical_and(i == mine, j == side)

            @pl.when(own)
            def _():
                pltpu.make_async_copy(src, gbuf.at[me], own_sem.at[1]).start()

            @pl.when(jnp.logical_not(own))
            def _():
                pltpu.make_async_remote_copy(
                    src_ref=src, dst_ref=gbuf.at[me],
                    send_sem=send_sem.at[2], recv_sem=recv_sem.at[2],
                    device_id=(i, j), device_id_type=MESH,
                ).start()

    partial((0,))
    correct(0)
    for j in range(groups):

        @pl.loop(0, side_parts)
        def _(n):
            rows = pl.ds(pl.multiple_of(n * prows, prows), prows)
            mbuf[j, rows] = feature(0, j * side_parts + n).astype(BF16)

    def send_query(d, carry):
        j = lax.rem(side + d, groups)
        pltpu.make_async_remote_copy(
            src_ref=mbuf.at[j], dst_ref=qland.at[side],
            send_sem=send_sem.at[3], recv_sem=recv_sem.at[3],
            device_id=(mine, j), device_id_type=MESH,
        ).start()
        return carry

    lax.fori_loop(1, groups, send_query, 0)
    own_q = pltpu.make_async_copy(mbuf.at[side], qland.at[side], own_sem.at[2])
    own_q.start()

    half = devices * chans

    def dot(left, right):
        return jnp.dot(left, right, preferred_element_type=F32)

    def part(value, c):
        return value[:, c * width : (c + 1) * width]

    def forward(source):
        spread[...] = source[...].astype(F32).reshape(half, width)
        columns = jnp.concatenate(
            [
                spread[pl.ds(c, devices, stride=chans), :].astype(BF16)
                for c in range(chans)
            ],
            axis=1,
        )
        first = dot(fwd[...], columns)
        cos, sin = twist[0], twist[1]
        rows = []
        for c in range(chans):
            real, imag = part(first[:devices], c), part(first[devices:], c)
            rows.append(
                jnp.concatenate(
                    [
                        (real * cos + imag * sin).astype(BF16),
                        (imag * cos - real * sin).astype(BF16),
                    ],
                    axis=1,
                )
            )
        return dot(jnp.concatenate(rows, axis=0), wide[0])

    for load in loads[4:]:
        load.wait()
    own_f.wait()
    got_f = fbuf.at[pl.ds(0, devices - groups)]
    pltpu.make_async_copy(got_f, got_f, recv_sem.at[1]).wait()
    hspec[...] = forward(fbuf)

    gated = gbuf.at[pl.ds(0, devices - 1)]
    pltpu.make_async_copy(gsend.at[pl.ds(0, chans)], gbuf.at[me], own_sem.at[1]).wait()
    pltpu.make_async_copy(gated, gated, recv_sem.at[2]).wait()

    spec = forward(gbuf)
    sr, si = part(spec, 0), part(spec, 1)
    fr, fi = hspec[:, :width], hspec[:, width:]
    prod = jnp.concatenate(
        [(sr * fr - si * fi).astype(BF16), (sr * fi + si * fr).astype(BF16)], axis=1
    )
    back = dot(prod, wide[1])
    cos, sin = twist[0], twist[1]
    columns = []
    for c in range(chans):
        rows = back[c * devices : (c + 1) * devices]
        br, bi = part(rows, 0), part(rows, 1)
        columns.append(
            jnp.concatenate(
                [(br * cos - bi * sin).astype(BF16), (br * sin + bi * cos).astype(BF16)],
                axis=0,
            )
        )
    conv = dot(inv[...], jnp.concatenate(columns, axis=1))
    for c in range(chans):
        spread[pl.ds(c, devices, stride=chans), :] = part(conv, c)
    fbuf[...] = (
        spread[...].reshape(devices, chans, width)
        + skipb[...] * gbuf[...].astype(F32)
    ).astype(BF16)

    def send_out(d, carry):
        i = lax.rem(mine + d, lanes)
        pltpu.make_async_remote_copy(
            src_ref=fbuf.at[pl.ds(i * groups, groups)],
            dst_ref=landed.at[:, side_rows(mine)],
            send_sem=send_sem.at[4], recv_sem=recv_sem.at[4],
            device_id=(i, side), device_id_type=MESH,
        ).start()
        return carry

    lax.fori_loop(1, lanes, send_out, 0)
    own_o = pltpu.make_async_copy(
        fbuf.at[pl.ds(mine * groups, groups)], landed.at[:, side_rows(mine)], own_sem.at[3]
    )
    own_o.start()

    @pl.when(me < devices - 1)
    def _():
        halo_copy(after).wait_send()

    sent_f = fbuf.at[pl.ds(0, devices - groups)]
    pltpu.make_async_copy(sent_f, sent_f, send_sem.at[1]).wait()
    pltpu.make_async_copy(gated, gated, send_sem.at[2]).wait()
    others = qland.at[pl.ds(0, groups - 1)]
    pltpu.make_async_copy(others, others, send_sem.at[3]).wait()
    pltpu.make_async_copy(others, others, recv_sem.at[3]).wait()
    own_q.wait()
    pltpu.make_async_copy(sent_f, sent_f, send_sem.at[4]).wait()
    own_o.wait()
    pltpu.make_async_copy(sent_f, sent_f, recv_sem.at[4]).wait()
    for g in range(groups):
        out[:, g * width : (g + 1) * width] = (
            qland[g].astype(F32) * landed[g].astype(F32)
        ).astype(BF16)


def fused_local(lanes, groups, qkv, conv_taps, filters, skip):
    devices = lanes * groups
    channels, width = qkv.shape[1], qkv.shape[2]
    chans = channels // devices
    count = conv_taps.shape[2]
    fwd, inv, wide, twist = tables(devices, width)
    hbm = pl.BlockSpec(memory_space=pltpu.HBM)
    vmem = pl.BlockSpec(memory_space=pltpu.VMEM)
    per_side = lanes * chans
    halo = (3, channels * 8 // width, width)
    return pl.pallas_call(
        functools.partial(kernel, lanes, groups, count - 1),
        out_shape=pltpu.VMEM((per_side, groups * width), BF16),
        in_specs=[hbm] * 8,
        out_specs=vmem,
        scratch_shapes=[
            pltpu.VMEM(qkv.shape, BF16),
            pltpu.VMEM(filters.shape, F32),
            pltpu.VMEM((3, count, channels), F32),
            pltpu.VMEM((1, per_side), F32),
            pltpu.VMEM(fwd.shape, BF16),
            pltpu.VMEM(inv.shape, BF16),
            pltpu.VMEM(wide.shape, BF16),
            pltpu.VMEM(twist.shape, F32),
            pltpu.VMEM(halo, BF16),
            pltpu.VMEM(halo, BF16),
            pltpu.VMEM((3, channels, width), F32),
            pltpu.VMEM((3, count - 1, halo[1], width), F32),
            pltpu.VMEM(halo, F32),
            pltpu.VMEM((3, channels, width), F32),
            pltpu.VMEM((chans, width), F32),
            pltpu.VMEM((groups, per_side, width), BF16),
            pltpu.VMEM((devices, chans, width), BF16),
            pltpu.VMEM((channels, width), BF16),
            pltpu.VMEM((devices, chans, width), BF16),
            pltpu.VMEM((groups, per_side, width), BF16),
            pltpu.VMEM((channels, 2 * width), F32),
            pltpu.VMEM((channels, width), F32),
            pltpu.VMEM((groups, per_side, width), BF16),
            pltpu.VMEM((groups, per_side, width), BF16),
            pltpu.SemaphoreType.DMA((8,)),
            pltpu.SemaphoreType.DMA((4,)),
            pltpu.SemaphoreType.DMA((5,)),
            pltpu.SemaphoreType.DMA((5,)),
        ],
        compiler_params=pltpu.CompilerParams(
            collective_id=0, has_side_effects=True, vmem_limit_bytes=24 * 1024 * 1024
        ),
    )(
        *(
            pltpu.with_memory_space_constraint(operand, pltpu.HBM)
            for operand in (
                qkv, conv_taps.transpose(0, 2, 1), filters, skip.reshape(1, -1),
                fwd, inv, wide, twist,
            )
        )
    )


def from_behind(shard, axis, by):
    length = lax.axis_size(axis)
    pairs = [(i, i + by) for i in range(length) if 0 <= i + by < length]
    return lax.ppermute(shard, axis, pairs)


def featurize(block, earlier, taps):
    reach = taps.shape[2] - 1
    length = block.shape[2]
    joined = jnp.concatenate([earlier, block], axis=2).astype(jnp.float32)
    total = jnp.zeros(block.shape, jnp.float32)
    for offset in range(taps.shape[2]):
        total = (
            total
            + taps[:, :, offset : offset + 1]
            * joined[:, :, reach - offset : reach - offset + length]
        )
    query = lax.optimization_barrier(total[0].astype(jnp.bfloat16))
    gated = lax.optimization_barrier((total[1] * total[2]).astype(jnp.bfloat16))
    return (query, gated)


def phase(product, modulus, sign):
    angle = sign * 2.0 * math.pi / modulus * (product % modulus).astype(jnp.float32)
    return (jnp.cos(angle), jnp.sin(angle))


def dft_table(index_in, index_out, modulus, sign):
    cosine, sine = phase(index_in[:, None] * index_out[None, :], modulus, sign)
    return jnp.stack([jnp.stack([cosine, sine]), jnp.stack([-sine, cosine])])


def complex_times(left, right):
    return jnp.stack(
        [left[0] * right[0] - left[1] * right[1], left[0] * right[1] + left[1] * right[0]]
    )


def twisted(values, cosine, sine):
    return jnp.stack([values[0] * cosine - values[1] * sine, values[0] * sine + values[1] * cosine])


def local_transform(values, sign):
    highest = lax.Precision.HIGHEST
    length = values.shape[-1]
    first = max((d for d in range(1, math.isqrt(length) + 1) if length % d == 0))
    second = length // first
    lead = values.shape[:-1]
    shaped = values.reshape(lead + (first, second))
    index_a = jnp.arange(first, dtype=jnp.int32)
    index_b = jnp.arange(second, dtype=jnp.int32)
    outer = dft_table(index_a, index_a, first, sign)
    part = jnp.einsum("p...ab,pqak->q...kb", shaped, outer, precision=highest)
    twist_c, twist_s = phase(index_a[:, None] * index_b[None, :], length, sign)
    part = twisted(part, twist_c, twist_s)
    inner = dft_table(index_b, index_b, second, sign)
    result = jnp.einsum("p...kb,pqbm->q...mk", part, inner, precision=highest)
    return result.reshape(lead + (length,))


def to_columns(values):
    return lax.all_to_all(
        values.astype(jnp.bfloat16), "ctx", split_axis=3, concat_axis=2, tiled=True
    ).astype(values.dtype)


def to_rows(values):
    return lax.all_to_all(
        values.astype(jnp.bfloat16), "ctx", split_axis=2, concat_axis=3, tiled=True
    ).astype(values.dtype)


def spread_conv(signal, filters):
    highest = lax.Precision.HIGHEST
    lanes = lax.axis_size("ctx")
    block = signal.shape[1]
    piece = block // lanes
    total_len = 2 * lanes * block
    mine = lax.axis_index("ctx")
    order = jnp.arange(2 * lanes, dtype=jnp.int32)
    owner = order // 2
    parity = order % 2
    freq_rows = jnp.where(
        owner == 0, parity * lanes, jnp.where(parity == 0, owner, 2 * lanes - owner)
    )
    own_rows = lax.dynamic_slice_in_dim(freq_rows, 2 * mine, 2)
    sources = jnp.arange(lanes, dtype=jnp.int32)
    cross = dft_table(sources, freq_rows, 2 * lanes, -1.0)
    column_pos = mine * piece + jnp.arange(piece, dtype=jnp.int32)
    twist_c, twist_s = phase(freq_rows[:, None] * column_pos[None, :], total_len, -1.0)
    columns = to_columns(jnp.stack([signal, filters])[:, :, None, :])
    spec = jnp.einsum("scaj,qar->qscrj", columns, cross[0], precision=highest)
    spec = twisted(spec, twist_c, twist_s)
    width_dev = spec.shape[2]
    arrived = to_rows(spec.reshape((4, width_dev) + spec.shape[3:]))
    arrived = arrived.reshape((2, 2, width_dev) + arrived.shape[2:])
    freq = local_transform(arrived, -1.0)
    prod = complex_times(freq[:, 0], freq[:, 1])
    back = local_transform(prod, 1.0)
    full_pos = jnp.arange(block, dtype=jnp.int32)
    turn_c, turn_s = phase(own_rows[:, None] * full_pos[None, :], total_len, 1.0)
    back = twisted(back, turn_c, turn_s)
    spread = to_columns(back)
    merge = dft_table(freq_rows, sources, 2 * lanes, 1.0)
    partial_out = jnp.einsum("pcrj,pra->caj", spread, merge[:, 0], precision=highest)
    landed = to_rows(partial_out[None])
    return landed[0, :, 0, :] / total_len


def local(qkv, conv_taps, filters, skip):
    reach = conv_taps.shape[2] - 1
    grouped = lax.all_to_all(qkv, "ch", split_axis=1, concat_axis=2, tiled=True)
    earlier = from_behind(grouped[:, :, -reach:], "ctx", 1)
    width_dev = grouped.shape[1]
    taps_mine = lax.dynamic_slice_in_dim(conv_taps, lax.axis_index("ch") * width_dev, width_dev, 1)
    query, gated = featurize(grouped, earlier, taps_mine)
    signal = gated.astype(jnp.float32)
    long_conv = spread_conv(signal, filters)
    mixed = query.astype(jnp.float32) * (long_conv + skip[:, None] * signal)
    return mixed.astype(jnp.bfloat16)


def solution(mesh):
    lanes, groups = mesh.shape["ctx"], mesh.shape["ch"]

    def body(qkv, conv_taps, filters, skip):
        chans = qkv.shape[1] // (lanes * groups)
        fits = (
            chans % 16 == 0
            and qkv.shape[2] == 128
            and (qkv.shape[1] // 16) % chans == 0
            and (lanes * chans) % (qkv.shape[1] // 16) == 0
            and (lanes * groups) % 16 == 0
            and conv_taps.shape[2] <= 8
        )
        if fits:
            return fused_local(lanes, groups, qkv, conv_taps, filters, skip)
        return local(qkv, conv_taps, filters, skip)

    return jax.shard_map(
        body,
        mesh=mesh,
        in_specs=(P(None, None, ("ctx", "ch")), P(), P("ch", "ctx"), P("ch")),
        out_specs=P("ch", "ctx"),
        check_vma=False,
    )
```

```python
import functools
import math

import jax
import jax.numpy as jnp
import ml_dtypes
import numpy as np
from jax import lax
from jax.experimental import pallas as pl
from jax.experimental.pallas import tpu as pltpu
from jax.sharding import PartitionSpec as P

MESH = pl.DeviceIdType.MESH
F32 = jnp.float32
BF16 = jnp.bfloat16


def tables(devices, width):
    total = 2 * devices * width
    a = np.arange(devices)
    k1 = np.arange(devices) + 0.5
    angle = 2 * np.pi * np.outer(k1, a) / (2 * devices)
    forward = np.concatenate([np.cos(angle), -np.sin(angle)], 0)
    inverse = np.concatenate([np.cos(angle.T), -np.sin(angle.T)], 1) * (2.0 / total)
    b = np.arange(width)
    turn = 2 * np.pi * np.outer(k1, b) / total
    twist = np.stack([np.cos(turn), np.sin(turn)])
    inner = 2 * np.pi * (np.outer(b, b) % width) / width
    cos, sin = np.cos(inner), np.sin(inner)
    wide = np.stack(
        [np.block([[cos, -sin], [sin, cos]]), np.block([[cos, sin], [-sin, cos]])]
    )
    low = lambda x: jnp.asarray(x.astype(ml_dtypes.bfloat16))
    return low(forward), low(inverse), low(wide), jnp.asarray(twist.astype(np.float32))


def kernel(
    lanes, groups, reach,
    qkv, taps, filters, skip, fwd_hbm, inv_hbm, wide_hbm, twist_hbm,
    out,
    qin, fraw, tapv, skipv, fwd, inv, wide, twist,
    halo_out, halo_in, tapc, ptaps, fixes, feat, skipb,
    fsend, fbuf, gsend, gbuf, qland, hspec, spread, mbuf, landed,
    load_sem, own_sem, send_sem, recv_sem,
):
    devices = lanes * groups
    chans, width = fbuf.shape[1], fbuf.shape[2]
    channels = qin.shape[1]
    mine = lax.axis_index("ctx")
    side = lax.axis_index("ch")
    me = mine * groups + side
    per_side = lanes * chans

    def side_rows(i):
        return pl.ds(pl.multiple_of(i * chans, chans), chans)

    loads = [
        pltpu.make_async_copy(src, dst, load_sem.at[n])
        for n, (src, dst) in enumerate(
            [
                (qkv, qin), (filters, fraw), (taps, tapv), (skip, skipv), (fwd_hbm, fwd),
                (wide_hbm, wide), (twist_hbm, twist), (inv_hbm, inv),
            ]
        )
    ]
    for load in loads:
        load.start()

    barrier = pltpu.get_barrier_semaphore()

    def greet(d, carry):
        t = lax.rem(me + d, devices)
        pl.semaphore_signal(
            barrier, inc=1, device_id=(t // groups, t % groups), device_id_type=MESH
        )
        return carry

    lax.fori_loop(1, devices, greet, 0)

    keep = 8
    parts = width // keep
    prows = channels // parts
    lane = lax.broadcasted_iota(jnp.int32, (prows, width), 1)
    loads[0].wait()
    for s in range(3):
        packed = jnp.zeros((prows, width), F32)
        for g in range(parts):
            rows = qin[s, g * prows : (g + 1) * prows].astype(F32)
            moved = pltpu.roll(rows, (keep * (g + 1)) % width, 1)
            packed = jnp.where((lane >= keep * g) & (lane < keep * (g + 1)), moved, packed)
        halo_out[s] = packed.astype(BF16)
    loads[1].wait()
    for g in range(groups):
        fsend[g] = fraw[:, g * width : (g + 1) * width].astype(BF16)

    pl.semaphore_wait(barrier, devices - 1)

    after, before = me + 1, me - 1

    def halo_copy(t):
        return pltpu.make_async_remote_copy(
            src_ref=halo_out, dst_ref=halo_in,
            send_sem=send_sem.at[0], recv_sem=recv_sem.at[0],
            device_id=(t // groups, t % groups), device_id_type=MESH,
        )

    @pl.when(me < devices - 1)
    def _():
        halo_copy(after).start()

    def near(d):
        return (2 * (d % 2) - 1) * ((d + 1) // 2)

    def send_filters(d, carry):
        i = lax.rem(mine + lanes + near(d), lanes)
        pltpu.make_async_remote_copy(
            src_ref=fsend.at[:, side_rows(i)],
            dst_ref=fbuf.at[pl.ds(mine * groups, groups)],
            send_sem=send_sem.at[1], recv_sem=recv_sem.at[1],
            device_id=(i, side), device_id_type=MESH,
        ).start()
        return carry

    lax.fori_loop(1, lanes, send_filters, 0)
    own_f = pltpu.make_async_copy(
        fsend.at[:, side_rows(mine)], fbuf.at[pl.ds(mine * groups, groups)], own_sem.at[0]
    )
    own_f.start()

    loads[2].wait()
    for s in range(3):
        wide_taps = jnp.concatenate(
            [tapv[s], jnp.zeros((width - reach - 1, channels), F32)], axis=0
        )
        tapc[s] = wide_taps.T

    spot = lax.rem(lane, keep)
    ptaps[...] = jnp.zeros_like(ptaps)

    def partial(streams):
        @pl.loop(0, parts)
        def _(g):
            rows = pl.ds(pl.multiple_of(g * prows, prows), prows)
            here = (lane >= keep * g) & (lane < keep * (g + 1))
            for s in streams:
                columns = tapc[s, rows]
                cur = qin[s, rows].astype(F32)
                acc = columns[:, :1] * cur
                for i in range(1, reach + 1):
                    tap = jnp.broadcast_to(columns[:, i : i + 1], (prows, width))
                    acc = acc + jnp.where(lane >= i, tap * pltpu.roll(cur, i, 1), 0.0)
                    ptaps[s, i - 1] = jnp.where(here & (spot < i), tap, ptaps[s, i - 1])
                feat[s, rows] = acc

    partial((1, 2))

    pick = lax.broadcasted_iota(jnp.int32, (chans, per_side), 1) == (
        mine * chans + lax.broadcasted_iota(jnp.int32, (chans, per_side), 0)
    )
    loads[3].wait()
    column = jnp.sum(jnp.where(pick, skipv[...], 0.0), axis=1, keepdims=True)
    skipb[...] = jnp.broadcast_to(column, (chans, width))

    @pl.when(me > 0)
    def _():
        halo_copy(before).wait_recv()

    @pl.when(me == 0)
    def _():
        halo_in[...] = jnp.zeros_like(halo_in)

    def correct(s):
        tail = halo_in[s].astype(F32)
        total = jnp.zeros((prows, width), F32)
        for i in range(1, reach + 1):
            total = total + ptaps[s, i - 1] * pltpu.roll(tail, width - keep + i, 1)
        fixes[s] = total

    def feature(stream, g):
        rows = pl.ds(pl.multiple_of(g * prows, prows), prows)
        more = pltpu.roll(fixes[stream], lax.rem(width - keep * g, width), 1)
        return feat[stream, rows] + jnp.where(lane < keep, more, 0.0)

    correct(1)
    correct(2)
    fold = prows // chans
    side_parts = per_side // prows

    @pl.loop(0, parts)
    def _(n):
        g = lax.rem(n + me // fold, parts)
        gate = (feature(1, g) * feature(2, g)).astype(BF16)
        gsend[pl.ds(pl.multiple_of(g * prows, prows), prows)] = gate
        j = g // side_parts
        for f in range(fold):
            i = (g % side_parts) * fold + f
            src = gsend.at[pl.ds(pl.multiple_of(g * prows + f * chans, chans), chans)]
            own = jnp.logical_and(i == mine, j == side)

            @pl.when(own)
            def _():
                pltpu.make_async_copy(src, gbuf.at[me], own_sem.at[1]).start()

            @pl.when(jnp.logical_not(own))
            def _():
                pltpu.make_async_remote_copy(
                    src_ref=src, dst_ref=gbuf.at[me],
                    send_sem=send_sem.at[2], recv_sem=recv_sem.at[2],
                    device_id=(i, j), device_id_type=MESH,
                ).start()

    partial((0,))
    correct(0)
    for j in range(groups):

        @pl.loop(0, side_parts)
        def _(n):
            rows = pl.ds(pl.multiple_of(n * prows, prows), prows)
            mbuf[j, rows] = feature(0, j * side_parts + n).astype(BF16)

    def send_query(d, carry):
        j = lax.rem(side + d, groups)
        pltpu.make_async_remote_copy(
            src_ref=mbuf.at[j], dst_ref=qland.at[side],
            send_sem=send_sem.at[3], recv_sem=recv_sem.at[3],
            device_id=(mine, j), device_id_type=MESH,
        ).start()
        return carry

    lax.fori_loop(1, groups, send_query, 0)
    own_q = pltpu.make_async_copy(mbuf.at[side], qland.at[side], own_sem.at[2])
    own_q.start()

    half = devices * chans

    def dot(left, right):
        return jnp.dot(left, right, preferred_element_type=F32)

    def part(value, c):
        return value[:, c * width : (c + 1) * width]

    def forward(source):
        spread[...] = source[...].astype(F32).reshape(half, width)
        columns = jnp.concatenate(
            [
                spread[pl.ds(c, devices, stride=chans), :].astype(BF16)
                for c in range(chans)
            ],
            axis=1,
        )
        first = dot(fwd[...], columns)
        cos, sin = twist[0], twist[1]
        rows = []
        for c in range(chans):
            real, imag = part(first[:devices], c), part(first[devices:], c)
            rows.append(
                jnp.concatenate(
                    [
                        (real * cos + imag * sin).astype(BF16),
                        (imag * cos - real * sin).astype(BF16),
                    ],
                    axis=1,
                )
            )
        return dot(jnp.concatenate(rows, axis=0), wide[0])

    for load in loads[4:]:
        load.wait()
    own_f.wait()
    got_f = fbuf.at[pl.ds(0, devices - groups)]
    pltpu.make_async_copy(got_f, got_f, recv_sem.at[1]).wait()
    hspec[...] = forward(fbuf)

    gated = gbuf.at[pl.ds(0, devices - 1)]
    pltpu.make_async_copy(gsend.at[pl.ds(0, chans)], gbuf.at[me], own_sem.at[1]).wait()
    pltpu.make_async_copy(gated, gated, recv_sem.at[2]).wait()

    spec = forward(gbuf)
    sr, si = part(spec, 0), part(spec, 1)
    fr, fi = hspec[:, :width], hspec[:, width:]
    prod = jnp.concatenate(
        [(sr * fr - si * fi).astype(BF16), (sr * fi + si * fr).astype(BF16)], axis=1
    )
    back = dot(prod, wide[1])
    cos, sin = twist[0], twist[1]
    columns = []
    for c in range(chans):
        rows = back[c * devices : (c + 1) * devices]
        br, bi = part(rows, 0), part(rows, 1)
        columns.append(
            jnp.concatenate(
                [(br * cos - bi * sin).astype(BF16), (br * sin + bi * cos).astype(BF16)],
                axis=0,
            )
        )
    conv = dot(inv[...], jnp.concatenate(columns, axis=1))
    for c in range(chans):
        spread[pl.ds(c, devices, stride=chans), :] = part(conv, c)
    fbuf[...] = (
        spread[...].reshape(devices, chans, width)
        + skipb[...] * gbuf[...].astype(F32)
    ).astype(BF16)

    def send_out(d, carry):
        i = lax.rem(mine + lanes + near(d), lanes)
        pltpu.make_async_remote_copy(
            src_ref=fbuf.at[pl.ds(i * groups, groups)],
            dst_ref=landed.at[:, side_rows(mine)],
            send_sem=send_sem.at[4], recv_sem=recv_sem.at[4],
            device_id=(i, side), device_id_type=MESH,
        ).start()
        return carry

    lax.fori_loop(1, lanes, send_out, 0)
    own_o = pltpu.make_async_copy(
        fbuf.at[pl.ds(mine * groups, groups)], landed.at[:, side_rows(mine)], own_sem.at[3]
    )
    own_o.start()

    @pl.when(me < devices - 1)
    def _():
        halo_copy(after).wait_send()

    sent_f = fbuf.at[pl.ds(0, devices - groups)]
    pltpu.make_async_copy(sent_f, sent_f, send_sem.at[1]).wait()
    pltpu.make_async_copy(gated, gated, send_sem.at[2]).wait()
    others = qland.at[pl.ds(0, groups - 1)]
    pltpu.make_async_copy(others, others, send_sem.at[3]).wait()
    pltpu.make_async_copy(others, others, recv_sem.at[3]).wait()
    own_q.wait()
    pltpu.make_async_copy(sent_f, sent_f, send_sem.at[4]).wait()
    own_o.wait()
    pltpu.make_async_copy(sent_f, sent_f, recv_sem.at[4]).wait()
    for g in range(groups):
        out[:, g * width : (g + 1) * width] = (
            qland[g].astype(F32) * landed[g].astype(F32)
        ).astype(BF16)


def fused_local(lanes, groups, qkv, conv_taps, filters, skip):
    devices = lanes * groups
    channels, width = qkv.shape[1], qkv.shape[2]
    chans = channels // devices
    count = conv_taps.shape[2]
    fwd, inv, wide, twist = tables(devices, width)
    hbm = pl.BlockSpec(memory_space=pltpu.HBM)
    vmem = pl.BlockSpec(memory_space=pltpu.VMEM)
    per_side = lanes * chans
    halo = (3, channels * 8 // width, width)
    return pl.pallas_call(
        functools.partial(kernel, lanes, groups, count - 1),
        out_shape=pltpu.VMEM((per_side, groups * width), BF16),
        in_specs=[hbm] * 8,
        out_specs=vmem,
        scratch_shapes=[
            pltpu.VMEM(qkv.shape, BF16),
            pltpu.VMEM(filters.shape, F32),
            pltpu.VMEM((3, count, channels), F32),
            pltpu.VMEM((1, per_side), F32),
            pltpu.VMEM(fwd.shape, BF16),
            pltpu.VMEM(inv.shape, BF16),
            pltpu.VMEM(wide.shape, BF16),
            pltpu.VMEM(twist.shape, F32),
            pltpu.VMEM(halo, BF16),
            pltpu.VMEM(halo, BF16),
            pltpu.VMEM((3, channels, width), F32),
            pltpu.VMEM((3, count - 1, halo[1], width), F32),
            pltpu.VMEM(halo, F32),
            pltpu.VMEM((3, channels, width), F32),
            pltpu.VMEM((chans, width), F32),
            pltpu.VMEM((groups, per_side, width), BF16),
            pltpu.VMEM((devices, chans, width), BF16),
            pltpu.VMEM((channels, width), BF16),
            pltpu.VMEM((devices, chans, width), BF16),
            pltpu.VMEM((groups, per_side, width), BF16),
            pltpu.VMEM((channels, 2 * width), F32),
            pltpu.VMEM((channels, width), F32),
            pltpu.VMEM((groups, per_side, width), BF16),
            pltpu.VMEM((groups, per_side, width), BF16),
            pltpu.SemaphoreType.DMA((8,)),
            pltpu.SemaphoreType.DMA((4,)),
            pltpu.SemaphoreType.DMA((5,)),
            pltpu.SemaphoreType.DMA((5,)),
        ],
        compiler_params=pltpu.CompilerParams(
            collective_id=0, has_side_effects=True, vmem_limit_bytes=24 * 1024 * 1024
        ),
    )(
        *(
            pltpu.with_memory_space_constraint(operand, pltpu.HBM)
            for operand in (
                qkv, conv_taps.transpose(0, 2, 1), filters, skip.reshape(1, -1),
                fwd, inv, wide, twist,
            )
        )
    )


def from_behind(shard, axis, by):
    length = lax.axis_size(axis)
    pairs = [(i, i + by) for i in range(length) if 0 <= i + by < length]
    return lax.ppermute(shard, axis, pairs)


def featurize(block, earlier, taps):
    reach = taps.shape[2] - 1
    length = block.shape[2]
    joined = jnp.concatenate([earlier, block], axis=2).astype(jnp.float32)
    total = jnp.zeros(block.shape, jnp.float32)
    for offset in range(taps.shape[2]):
        total = (
            total
            + taps[:, :, offset : offset + 1]
            * joined[:, :, reach - offset : reach - offset + length]
        )
    query = lax.optimization_barrier(total[0].astype(jnp.bfloat16))
    gated = lax.optimization_barrier((total[1] * total[2]).astype(jnp.bfloat16))
    return (query, gated)


def phase(product, modulus, sign):
    angle = sign * 2.0 * math.pi / modulus * (product % modulus).astype(jnp.float32)
    return (jnp.cos(angle), jnp.sin(angle))


def dft_table(index_in, index_out, modulus, sign):
    cosine, sine = phase(index_in[:, None] * index_out[None, :], modulus, sign)
    return jnp.stack([jnp.stack([cosine, sine]), jnp.stack([-sine, cosine])])


def complex_times(left, right):
    return jnp.stack(
        [left[0] * right[0] - left[1] * right[1], left[0] * right[1] + left[1] * right[0]]
    )


def twisted(values, cosine, sine):
    return jnp.stack([values[0] * cosine - values[1] * sine, values[0] * sine + values[1] * cosine])


def local_transform(values, sign):
    highest = lax.Precision.HIGHEST
    length = values.shape[-1]
    first = max((d for d in range(1, math.isqrt(length) + 1) if length % d == 0))
    second = length // first
    lead = values.shape[:-1]
    shaped = values.reshape(lead + (first, second))
    index_a = jnp.arange(first, dtype=jnp.int32)
    index_b = jnp.arange(second, dtype=jnp.int32)
    outer = dft_table(index_a, index_a, first, sign)
    part = jnp.einsum("p...ab,pqak->q...kb", shaped, outer, precision=highest)
    twist_c, twist_s = phase(index_a[:, None] * index_b[None, :], length, sign)
    part = twisted(part, twist_c, twist_s)
    inner = dft_table(index_b, index_b, second, sign)
    result = jnp.einsum("p...kb,pqbm->q...mk", part, inner, precision=highest)
    return result.reshape(lead + (length,))


def to_columns(values):
    return lax.all_to_all(
        values.astype(jnp.bfloat16), "ctx", split_axis=3, concat_axis=2, tiled=True
    ).astype(values.dtype)


def to_rows(values):
    return lax.all_to_all(
        values.astype(jnp.bfloat16), "ctx", split_axis=2, concat_axis=3, tiled=True
    ).astype(values.dtype)


def spread_conv(signal, filters):
    highest = lax.Precision.HIGHEST
    lanes = lax.axis_size("ctx")
    block = signal.shape[1]
    piece = block // lanes
    total_len = 2 * lanes * block
    mine = lax.axis_index("ctx")
    order = jnp.arange(2 * lanes, dtype=jnp.int32)
    owner = order // 2
    parity = order % 2
    freq_rows = jnp.where(
        owner == 0, parity * lanes, jnp.where(parity == 0, owner, 2 * lanes - owner)
    )
    own_rows = lax.dynamic_slice_in_dim(freq_rows, 2 * mine, 2)
    sources = jnp.arange(lanes, dtype=jnp.int32)
    cross = dft_table(sources, freq_rows, 2 * lanes, -1.0)
    column_pos = mine * piece + jnp.arange(piece, dtype=jnp.int32)
    twist_c, twist_s = phase(freq_rows[:, None] * column_pos[None, :], total_len, -1.0)
    columns = to_columns(jnp.stack([signal, filters])[:, :, None, :])
    spec = jnp.einsum("scaj,qar->qscrj", columns, cross[0], precision=highest)
    spec = twisted(spec, twist_c, twist_s)
    width_dev = spec.shape[2]
    arrived = to_rows(spec.reshape((4, width_dev) + spec.shape[3:]))
    arrived = arrived.reshape((2, 2, width_dev) + arrived.shape[2:])
    freq = local_transform(arrived, -1.0)
    prod = complex_times(freq[:, 0], freq[:, 1])
    back = local_transform(prod, 1.0)
    full_pos = jnp.arange(block, dtype=jnp.int32)
    turn_c, turn_s = phase(own_rows[:, None] * full_pos[None, :], total_len, 1.0)
    back = twisted(back, turn_c, turn_s)
    spread = to_columns(back)
    merge = dft_table(freq_rows, sources, 2 * lanes, 1.0)
    partial_out = jnp.einsum("pcrj,pra->caj", spread, merge[:, 0], precision=highest)
    landed = to_rows(partial_out[None])
    return landed[0, :, 0, :] / total_len


def local(qkv, conv_taps, filters, skip):
    reach = conv_taps.shape[2] - 1
    grouped = lax.all_to_all(qkv, "ch", split_axis=1, concat_axis=2, tiled=True)
    earlier = from_behind(grouped[:, :, -reach:], "ctx", 1)
    width_dev = grouped.shape[1]
    taps_mine = lax.dynamic_slice_in_dim(conv_taps, lax.axis_index("ch") * width_dev, width_dev, 1)
    query, gated = featurize(grouped, earlier, taps_mine)
    signal = gated.astype(jnp.float32)
    long_conv = spread_conv(signal, filters)
    mixed = query.astype(jnp.float32) * (long_conv + skip[:, None] * signal)
    return mixed.astype(jnp.bfloat16)


def solution(mesh):
    lanes, groups = mesh.shape["ctx"], mesh.shape["ch"]

    def body(qkv, conv_taps, filters, skip):
        chans = qkv.shape[1] // (lanes * groups)
        fits = (
            chans % 16 == 0
            and qkv.shape[2] == 128
            and (qkv.shape[1] // 16) % chans == 0
            and (lanes * chans) % (qkv.shape[1] // 16) == 0
            and (lanes * groups) % 16 == 0
            and conv_taps.shape[2] <= 8
        )
        if fits:
            return fused_local(lanes, groups, qkv, conv_taps, filters, skip)
        return local(qkv, conv_taps, filters, skip)

    return jax.shard_map(
        body,
        mesh=mesh,
        in_specs=(P(None, None, ("ctx", "ch")), P(), P("ch", "ctx"), P("ch")),
        out_specs=P("ch", "ctx"),
        check_vma=False,
    )
```
